256 devices in a mesh: ctx: 32 (over x, y, core), head: 8 (over z).
Axes of the slice: x: 4, y: 4, z: 8, core: 2. Of those that a mesh axis runs over, the one named last changes fastest.
Arguments:
- queries: bfloat16 [32768, 8, 128], P(('ctx', 'head')), may hold values from -4.5 to 4.5
- keys_in: bfloat16 [32768, 8, 128], P(('ctx', 'head')), may hold values from -4.5 to 4.5
- values: bfloat16 [32768, 8, 128], P(('ctx', 'head')), may hold values from -6 to 6
- grad_out: bfloat16 [32768, 8, 128], P(('ctx', 'head')), may hold values from -6 to 6
- slopes: float32 [8], replicated, may hold values from 6.1035156e-05 to 0.03125
- doc_lengths: int32 [16], replicated, may hold values from 1 to 4096, 32768 in all
Outputs:
- grad_query: bfloat16 [32768, 8, 128], P(('ctx', 'head'))
- grad_key: bfloat16 [32768, 8, 128], P(('ctx', 'head'))
- grad_value: bfloat16 [32768, 8, 128], P(('ctx', 'head'))
The draws below stay inside these ranges and needn't reach their ends.
Inputs may be any that keep to these rules, and one draw needn't show every extreme that they name: `doc_lengths`: the 16 lengths sum to 32768, and the longest is exactly 4096.
All inputs are finite; a program needn't handle non-finite values.
Results may differ from the reference program's by a relative error of at most 0.0075.
Values may be sent and summed in bfloat16 or wider, within the bound.
No kernel may reach another device: no remote copies, remote signals or barrier semaphores. Data moves between devices by JAX's collectives and lax.ppermute only.
A program may use at most 64 MiB of HBM per device.

```python
import math
import jax
import jax.numpy as jnp
import numpy as np
from jax import lax

HD = 128
HEADS = 8
DOCS = 16
TOK_DEV = 1024
SEQ = 32768
DOC_MAX = 4096
REACH = 4


def drawn_draw(key):
    return jnp.clip(jax.random.normal(jax.random.fold_in(key, 6), (SEQ, HEADS, HD), jnp.float32), -4.5, 4.5)


def draw_queries(key, part):
    drawn = drawn_draw(jax.random.fold_in(key, 11))
    return drawn.astype(jnp.bfloat16)


def draw_keys_in(key, part):
    drawn = drawn_draw(jax.random.fold_in(key, 13))
    return drawn.astype(jnp.bfloat16)


def block_levels(own_key, dims, pieces, smallest, top_value):
    gain = 1.0
    for dim, blocks in pieces:
        steps = jax.random.uniform(jax.random.fold_in(jax.random.fold_in(own_key, 6), dim), (blocks,), jnp.float32, smallest / len(pieces), top_value / len(pieces))
        gain = gain * jnp.repeat(jnp.exp(steps), dims[dim] // blocks).reshape((-1,) + (1,) * (len(dims) - 1 - dim))
    return gain


def length_profile(number_of, total, reach, skew):
    weights = [(1 << 20) // math.isqrt(grade ** skew) + 1 for grade in range(2, number_of + 1)]
    surplus, holding = total - reach - (number_of - 1), [1] * (number_of - 1)
    while surplus > 0:
        movable = [i for i in range(number_of - 1) if holding[i] < reach]
        pool, budget = sum([weights[i] for i in movable]), surplus
        for i in movable:
            addition = min(reach - holding[i], max(1, budget * weights[i] // pool), surplus)
            holding[i] = holding[i] + addition
            surplus = surplus - addition
    return np.array([reach] + holding)


def ragged_sizes(rng, amount, total, limit, skew):
    if amount == 2:
        one = jax.random.randint(rng, (), max(1, total - limit), min(limit, total - 1) + 1)
        return jnp.stack([one, total - one])
    sizes = jnp.asarray(length_profile(amount, total, limit, skew), jnp.int32)
    twos = (amount - 1) // 2
    donor, receiver = sizes[1:1 + 2 * twos:2], sizes[2:2 + 2 * twos:2]
    room = jnp.minimum(donor - 1, limit - receiver)
    shifted = jax.random.randint(jax.random.fold_in(rng, 1), (twos,), 0, 1 << 20) % (room + 1)
    sizes = sizes.at[1:1 + 2 * twos:2].set(donor - shifted).at[2:2 + 2 * twos:2].set(receiver + shifted)
    return sizes[jax.random.permutation(jax.random.fold_in(rng, 2), amount)]


def noise(key, shape, scale, limit, shards=(), held_as=jnp.bfloat16):
    drawn = jax.random.normal(key, shape, jnp.float32) * scale
    if len(shards) > 0:
        drawn = block_levels(key, shape, shards, -0.22, 0.18) * drawn
    return jnp.clip(drawn, min=-limit, max=limit).astype(held_as)


def setup_inputs(seed: int = 0) -> dict:
    splits = jax.random.split(jax.random.key(seed), 7)
    queries = draw_queries(jax.random.fold_in(splits[6], 71), 0)
    keys_in = draw_keys_in(jax.random.fold_in(splits[6], 71), 0)
    values = noise(splits[2], (SEQ, HEADS, HD), 1.0, 6.0, ((0, 256),))
    grad_out = noise(splits[3], (SEQ, HEADS, HD), 1.0, 6.0, ((0, 256),))
    slopes = jnp.clip(jnp.exp(jax.random.uniform(splits[4], (HEADS,), jnp.float32, math.log(6.103515625e-05), math.log(0.03125))), 6.103515625e-05, 0.03125)
    doc_lengths = ragged_sizes(splits[5], DOCS, SEQ, DOC_MAX, 2).astype(jnp.int32)
    return dict(queries=queries, keys_in=keys_in, values=values, grad_out=grad_out, slopes=slopes, doc_lengths=doc_lengths)


def reference(queries, keys_in, values, grad_out, slopes, doc_lengths):
    inv_scale = 1.0 / math.sqrt(HD)
    window = (REACH + 1) * TOK_DEV
    doc_ends = jnp.cumsum(doc_lengths).astype(jnp.int32)
    doc_starts = (doc_ends - doc_lengths).astype(jnp.int32)
    positions = jnp.arange(SEQ, dtype=jnp.int32)
    row_starts = lax.optimization_barrier(jnp.max(jnp.where(doc_starts[None, :] <= positions[:, None], doc_starts[None, :], 0), axis=1)).astype(jnp.int32)
    padding = jnp.zeros((REACH * TOK_DEV, HEADS, HD), keys_in.dtype)
    keys_pad = jnp.concatenate([padding, keys_in], axis=0)
    values_pad = jnp.concatenate([padding, values], axis=0)
    acc_zero = jnp.zeros((SEQ + REACH * TOK_DEV, HEADS, HD), jnp.float32)

    def block_step(carried, block_index):
        key_acc, value_acc = carried
        first_row = (block_index * TOK_DEV).astype(jnp.int32)
        q_block = lax.dynamic_slice_in_dim(queries, first_row, TOK_DEV, 0).astype(jnp.float32)
        g_block = lax.dynamic_slice_in_dim(grad_out, first_row, TOK_DEV, 0).astype(jnp.float32)
        k_window = lax.dynamic_slice_in_dim(keys_pad, first_row, window, 0).astype(jnp.float32)
        v_window = lax.dynamic_slice_in_dim(values_pad, first_row, window, 0).astype(jnp.float32)
        q_pos = first_row + jnp.arange(TOK_DEV, dtype=jnp.int32)
        k_pos = first_row - REACH * TOK_DEV + jnp.arange(window, dtype=jnp.int32)
        q_starts = lax.dynamic_slice_in_dim(row_starts, first_row, TOK_DEV, 0)
        raw = jnp.einsum('qhd,khd->hqk', q_block, k_window)
        distance = (q_pos[:, None] - k_pos[None, :]).astype(jnp.float32)
        scores = raw * inv_scale - slopes[:, None, None] * distance[None]
        allowed = ((k_pos[None, :] <= q_pos[:, None]) & (k_pos[None, :] >= q_starts[:, None]))[None]
        row_max = lax.optimization_barrier(jnp.max(jnp.where(allowed, scores, -1e+30), axis=2))
        row_sum = lax.optimization_barrier(jnp.sum(jnp.where(allowed, jnp.exp(scores - row_max[:, :, None]), 0.0), axis=2))
        log_total = row_max + jnp.log(row_sum)
        weights = jnp.where(allowed, jnp.exp(scores - log_total[:, :, None]), 0.0)
        weights_b = lax.optimization_barrier(weights.astype(jnp.bfloat16)).astype(jnp.float32)
        attn_out = jnp.einsum('hqk,khd->qhd', weights_b, v_window)
        row_delta = lax.optimization_barrier(jnp.sum(g_block * attn_out, axis=2)).T
        dweights = jnp.einsum('qhd,khd->hqk', g_block, v_window)
        dscores = weights * (dweights - row_delta[:, :, None])
        dscores_b = lax.optimization_barrier(dscores.astype(jnp.bfloat16)).astype(jnp.float32)
        grad_rows = (jnp.einsum('hqk,khd->qhd', dscores_b, k_window) * inv_scale).astype(jnp.bfloat16)
        key_term = jnp.einsum('hqk,qhd->khd', dscores_b, q_block)
        value_term = jnp.einsum('hqk,qhd->khd', weights_b, g_block)
        key_acc = lax.dynamic_update_slice_in_dim(key_acc, lax.dynamic_slice_in_dim(key_acc, first_row, window, 0) + key_term, first_row, 0)
        value_acc = lax.dynamic_update_slice_in_dim(value_acc, lax.dynamic_slice_in_dim(value_acc, first_row, window, 0) + value_term, first_row, 0)
        return ((key_acc, value_acc), grad_rows)
    (key_acc, value_acc), grad_blocks = lax.scan(block_step, (acc_zero, acc_zero), jnp.arange(SEQ // TOK_DEV, dtype=jnp.int32))
    grad_query = grad_blocks.reshape(SEQ, HEADS, HD)
    grad_key = (key_acc[REACH * TOK_DEV:] * inv_scale).astype(jnp.bfloat16)
    grad_value = value_acc[REACH * TOK_DEV:].astype(jnp.bfloat16)
    return (grad_query, grad_key, grad_value)
```

```python
import math

import jax
import jax.numpy as jnp
from jax import lax
from jax.experimental import pallas as pl
from jax.experimental.pallas import tpu as pltpu
from jax.sharding import PartitionSpec as P

TILE = 512
BLOCK = 1024
SLOTS = 6
NT = (((1,), (1,)), ((), ()))
NN = (((1,), (0,)), ((), ()))


def mm(a, b, dims):
    return lax.dot_general(a, b, dims, preferred_element_type=jnp.float32)


def attention_kernel(
    doc_ref, slope_ref, qg, *refs
):
    kvs = refs[:SLOTS]
    dq_ref = refs[SLOTS]
    outs = refs[SLOTS + 1 : 2 * SLOTS + 1]
    q_s, g_s, k_s, v_s, kt_s, dk_s, dv_s, s_s, p_s, m_s, sems = refs[2 * SLOTS + 1 :]
    block = lax.axis_index("ctx")
    core = block % 2
    base = (block - core) * BLOCK - 4 * BLOCK
    slope2 = slope_ref[lax.axis_index("head")] * math.log2(math.e)
    inv_scale = 1.0 / math.sqrt(128.0)
    scale2 = inv_scale * math.log2(math.e)

    def place(slot):
        pair = 4 - 2 * (slot // 2)
        return pair + (core if slot % 2 == 0 else 1 - core)

    copies = [
        pltpu.make_async_copy(qg.at[:, 0], q_s, sems.at[0]),
        pltpu.make_async_copy(qg.at[:, 1], g_s, sems.at[1]),
    ]
    for slot in range(SLOTS):
        rows = pl.ds(place(slot) * 8, 8)
        copies.append(
            pltpu.make_async_copy(kvs[slot].at[:, 0], k_s.at[rows], sems.at[2 + 2 * slot])
        )
        copies.append(
            pltpu.make_async_copy(kvs[slot].at[:, 1], v_s.at[rows], sems.at[3 + 2 * slot])
        )
    for copy in copies:
        copy.start()
    dk_s[...] = jnp.zeros_like(dk_s)
    dv_s[...] = jnp.zeros_like(dv_s)
    for copy in copies:
        copy.wait()

    starts = []
    at = jnp.int32(0)
    for d in range(16):
        starts.append(at)
        at = at + doc_ref[d]

    def start_of(pos):
        found = jnp.zeros_like(pos)
        for s in starts:
            found = jnp.where(pos >= s, s, found)
        return found

    def k_tile(ref, t):
        return ref[pl.ds(4 * t, 4)].reshape(TILE, 128)

    first = lax.shift_right_logical(start_of(block * BLOCK) - base, 9)
    last = (4 + core) * 2 + 2

    def transpose_keys(t, carry):
        kt_s[t] = k_tile(k_s, t).T
        return carry

    lax.fori_loop(first, last, transpose_keys, 0)

    row_bias = slope2 * lax.broadcasted_iota(jnp.int32, (TILE, 128), 0).astype(jnp.float32)

    def q_step(qt, carry):
        q0 = block * BLOCK + qt * TILE
        start0 = start_of(q0)
        start1 = start_of(q0 + TILE - 1)
        lo = lax.shift_right_logical(start0 - base, 9)
        hi = (4 + core) * 2 + qt + 1
        q_t = q_s[pl.ds(4 * qt, 4)].reshape(TILE, 128)
        g_t = g_s[pl.ds(4 * qt, 4)].reshape(TILE, 128)
        m_s[...] = jnp.full_like(m_s, -1e30)

        def score(t, c):
            k0 = base + t * TILE
            raw = mm(k_tile(k_s, t), q_t, NT)
            bias = row_bias + slope2 * (k0 - q0).astype(jnp.float32)
            s = raw * scale2 + jnp.concatenate([bias] * 4, axis=1)
            full = jnp.logical_and(k0 >= start1, k0 + TILE - 1 <= q0)

            def keep(s):
                s_s[t] = s
                m_s[...] = jnp.maximum(m_s[...], jnp.max(s.reshape(TILE // 8, 8, TILE), axis=0))

            @pl.when(full)
            def _():
                keep(s)

            @pl.when(jnp.logical_not(full))
            def _():
                q_pos = q0 + lax.broadcasted_iota(jnp.int32, (1, TILE), 1)
                low = start_of(q_pos) - k0
                k_pos = lax.broadcasted_iota(jnp.int32, (TILE, TILE), 0)
                allowed = jnp.logical_and(k_pos >= low, k_pos <= q_pos - k0)
                keep(jnp.where(allowed, s, -1e30))

            return c

        lax.fori_loop(lo, hi, score, 0)
        row_max = jnp.max(m_s[...], axis=0, keepdims=True)

        def weigh(t, c):
            total, delta = c
            dp = mm(k_tile(v_s, t), g_t, NT)
            p = jnp.exp2(s_s[t] - row_max)
            s_s[t] = p
            p_s[t] = dp
            total = total + jnp.sum(p.reshape(TILE // 8, 8, TILE), axis=0)
            delta = delta + jnp.sum((p * dp).reshape(TILE // 8, 8, TILE), axis=0)
            return total, delta

        zero = jnp.zeros((8, TILE), jnp.float32)
        total, delta = lax.fori_loop(lo, hi, weigh, (zero, zero))
        inv = 1.0 / jnp.sum(total, axis=0, keepdims=True)
        row_delta = jnp.sum(delta, axis=0, keepdims=True) * inv

        def grads(t, dq):
            w = s_s[t] * inv
            ds = (w * (p_s[t] - row_delta)).astype(jnp.bfloat16)
            dv_s[t] += mm(w.astype(jnp.bfloat16), g_t, NN)
            dk_s[t] += mm(ds, q_t, NN)
            return dq + mm(kt_s[t], ds, NN)

        dq = lax.fori_loop(lo, hi, grads, jnp.zeros((128, TILE), jnp.float32))
        dq = (dq * inv_scale).T.astype(jnp.bfloat16)
        dq_ref[pl.ds(4 * qt, 4)] = dq.reshape(4, 128, 128)
        return carry

    lax.fori_loop(0, 2, q_step, 0)

    for slot in range(SLOTS):
        for half in range(2):
            t = place(slot) * 2 + half
            rows = slice(4 * half, 4 * half + 4)
            outs[slot][rows, 0] = (
                (dk_s[t] * inv_scale).reshape(4, 128, 128).astype(outs[slot].dtype)
            )
            outs[slot][rows, 1] = dv_s[t].reshape(4, 128, 128).astype(outs[slot].dtype)


def attention(doc_lengths, slopes, qg, kvs):
    small = jax.ShapeDtypeStruct((8, 2, 128, 128), jnp.bfloat16)
    wide = jax.ShapeDtypeStruct((8, 2, 128, 128), jnp.float32)
    smem = pl.BlockSpec(memory_space=pltpu.SMEM)
    anywhere = pl.BlockSpec(memory_space=pl.ANY)
    vmem = pl.BlockSpec(memory_space=pltpu.VMEM)
    tiles = SLOTS * BLOCK // TILE
    return pl.pallas_call(
        attention_kernel,
        out_shape=(jax.ShapeDtypeStruct((8, 128, 128), jnp.bfloat16), wide) + (small,) * 5,
        in_specs=[smem, smem] + [anywhere] * 7,
        out_specs=(vmem,) * 7,
        scratch_shapes=[
            pltpu.VMEM((8, 128, 128), jnp.bfloat16),
            pltpu.VMEM((8, 128, 128), jnp.bfloat16),
            pltpu.VMEM((8 * SLOTS, 128, 128), jnp.bfloat16),
            pltpu.VMEM((8 * SLOTS, 128, 128), jnp.bfloat16),
            pltpu.VMEM((tiles, 128, TILE), jnp.bfloat16),
            pltpu.VMEM((tiles, TILE, 128), jnp.float32),
            pltpu.VMEM((tiles, TILE, 128), jnp.float32),
            pltpu.VMEM((tiles, TILE, TILE), jnp.float32),
            pltpu.VMEM((tiles, TILE, TILE), jnp.float32),
            pltpu.VMEM((8, TILE), jnp.float32),
            pltpu.SemaphoreType.DMA((2 + 2 * SLOTS,)),
        ],
        compiler_params=pltpu.CompilerParams(vmem_limit_bytes=56 * 1024 * 1024),
    )(doc_lengths, slopes, qg, *kvs)


def shifted(x, distance):
    n = lax.axis_size("ctx")
    return lax.ppermute(x, "ctx", [(i, (i + distance) % n) for i in range(n)])


def swapped(x):
    n = lax.axis_size("ctx")
    return lax.ppermute(x, "ctx", [(i, i ^ 1) for i in range(n)])


def to_heads(a, b):
    both = jnp.stack([a.transpose(1, 0, 2), b.transpose(1, 0, 2)], axis=1)
    return lax.all_to_all(both, "head", 0, 0, tiled=True)


def body(queries, keys_in, values, grad_out, slopes, doc_lengths):
    kv = to_heads(keys_in, values)
    qg = to_heads(queries, grad_out)
    kv_s = swapped(kv)
    kv1 = shifted(kv, 2)
    kv2 = shifted(kv, 4)
    kv1_s = swapped(kv1)
    kv2_s = swapped(kv2)
    dq, own, own_s, one, one_s, two, two_s = attention(
        doc_lengths, slopes, qg, (kv, kv_s, kv1, kv1_s, kv2, kv2_s)
    )
    own_r = swapped(own_s)
    one_r = swapped(one_s)
    two_r = swapped(two_s)
    f32 = jnp.float32
    two_t = (two.astype(f32) + two_r.astype(f32)).astype(jnp.bfloat16)
    one_t = (one.astype(f32) + one_r.astype(f32)).astype(jnp.bfloat16)
    back2 = shifted(two_t, -4)
    back1 = shifted(one_t, -2)
    dq = lax.all_to_all(dq, "head", 0, 0, tiled=True)
    dkv = own + own_r.astype(f32) + back1.astype(f32) + back2.astype(f32)
    dkv = lax.all_to_all(dkv.astype(jnp.bfloat16), "head", 0, 0, tiled=True)
    return (
        dq.transpose(1, 0, 2),
        dkv[:, 0].transpose(1, 0, 2),
        dkv[:, 1].transpose(1, 0, 2),
    )


def solution(mesh):
    placed = P(("ctx", "head"), None, None)
    return jax.shard_map(
        body,
        mesh=mesh,
        in_specs=(placed,) * 4 + (P(), P()),
        out_specs=(placed,) * 3,
        check_vma=False,
    )
```

```python
import math

import jax
import jax.numpy as jnp
from jax import lax
from jax.experimental import pallas as pl
from jax.experimental.pallas import tpu as pltpu
from jax.sharding import PartitionSpec as P

TILE = 512
CHUNK = 128
BLOCK = 1024
SLOTS = 6
TILES = 10
NT = (((1,), (1,)), ((), ()))
NN = (((1,), (0,)), ((), ()))


def mm(a, b, dims):
    return lax.dot_general(a, b, dims, preferred_element_type=jnp.float32)


def attention_kernel(doc_ref, slope_ref, qg, *refs):
    kvs = refs[:SLOTS]
    dq_ref, mine_ref, send_ref = refs[SLOTS : SLOTS + 3]
    q_s, g_s, k_s, v_s, qt_s, gt_s, s_s, p_s, m_s, total_s, delta_s, dq_s, sems = refs[SLOTS + 3 :]
    block = lax.axis_index("ctx")
    core = block % 2
    q0 = block * BLOCK
    base = q0 - 4 * BLOCK
    slope2 = slope_ref[lax.axis_index("head")] * math.log2(math.e)
    inv_scale = 1.0 / math.sqrt(128.0)
    scale2 = inv_scale * math.log2(math.e)

    starts = []
    at = jnp.int32(0)
    for d in range(16):
        starts.append(at)
        at = at + doc_ref[d]

    def start_of(pos):
        found = jnp.zeros_like(pos)
        for s in starts:
            found = jnp.where(pos >= s, s, found)
        return found

    start0, start1 = start_of(q0), start_of(q0 + BLOCK - 1)
    lo = lax.shift_right_logical(start0 - base, 9)
    hi = TILES

    def place(slot):
        pair = 2 * (slot % 3)
        return 4 - pair if slot < 3 else 4 - pair + 1 - 2 * core

    def needed(slot):
        at = place(slot)
        return jnp.logical_and(at <= 4, 2 * at + 2 > lo)

    q_copy = pltpu.make_async_copy(qg.at[:, 0], q_s, sems.at[0])
    g_copy = pltpu.make_async_copy(qg.at[:, 1], g_s, sems.at[1])

    def block_copies(slot):
        at = jnp.clip(place(slot), 0, 4)
        rows = pl.ds(at * 8, 8)
        return (
            pltpu.make_async_copy(kvs[slot].at[:, 0], k_s.at[rows], sems.at[2 + at]),
            pltpu.make_async_copy(kvs[slot].at[:, 1], v_s.at[rows], sems.at[7 + at]),
        )

    q_copy.start()
    g_copy.start()
    for slot in (0, 3, 1, 4, 2, 5):

        @pl.when(needed(slot))
        def _():
            for copy in block_copies(slot):
                copy.start()

    def arrived(at):
        rows = pl.ds(at * 8, 8)
        pltpu.make_async_copy(kvs[0].at[:, 0], k_s.at[rows], sems.at[2 + at]).wait()
        pltpu.make_async_copy(kvs[0].at[:, 1], v_s.at[rows], sems.at[7 + at]).wait()

    def k_tile(ref, t):
        return ref[pl.ds(4 * t, 4)].reshape(TILE, 128)

    row_bias = slope2 * lax.broadcasted_iota(jnp.int32, (TILE, 128), 0).astype(jnp.float32)
    pieces = [slice(i * CHUNK, (i + 1) * CHUNK) for i in range(TILE // CHUNK)]

    def folded(x, reduce):
        return reduce(x.reshape(CHUNK // 8, 8, BLOCK), axis=0)

    def masks(t):
        k0 = base + t * TILE
        q_pos = q0 + lax.broadcasted_iota(jnp.int32, (1, BLOCK), 1)
        return start_of(q_pos) - k0, q_pos - k0

    def scores(raw, t, rows, limits):
        offset = slope2 * (base + t * TILE - q0 - BLOCK // 2).astype(jnp.float32)
        bias = row_bias[rows] + offset
        s = raw[rows] * scale2 + jnp.concatenate([bias] * (BLOCK // 128), axis=1)
        if limits is None:
            return s
        k_pos = lax.broadcasted_iota(jnp.int32, (CHUNK, BLOCK), 0) + rows.start
        allowed = jnp.logical_and(k_pos >= limits[0], k_pos <= limits[1])
        return jnp.where(allowed, s, -1e30)

    def weigh(t, limits, top):
        raw = mm(k_tile(k_s, t), qt_s[...], NN)
        dp = mm(k_tile(v_s, t), gt_s[...], NN)
        total, delta = total_s[...], delta_s[...]
        for rows in pieces:
            s = scores(raw, t, rows, limits)
            p = jnp.exp2(s if top is None else s - top)
            s_s[t, rows] = p
            p_s[t, rows] = dp[rows]
            total = total + folded(p, jnp.sum)
            delta = delta + folded(p * dp[rows], jnp.sum)
        total_s[...] = total
        delta_s[...] = delta

    def clear():
        total_s[...] = jnp.zeros_like(total_s)
        delta_s[...] = jnp.zeros_like(delta_s)

    def first_pass(i, c):
        t = hi - 1 - i

        @pl.when(t % 2 == 1)
        def _():
            arrived(lax.shift_right_logical(t, 1))

        k0 = base + t * TILE
        full = jnp.logical_and(k0 >= start1, k0 + TILE - 1 <= q0)

        @pl.when(full)
        def _():
            weigh(t, None, None)

        @pl.when(jnp.logical_not(full))
        def _():
            weigh(t, masks(t), None)

        return c

    clear()
    dq_s[...] = jnp.zeros_like(dq_s)
    send_ref[2 * core] = jnp.zeros((8, 2, 128, 128), jnp.bfloat16)
    q_copy.wait()
    g_copy.wait()
    qt_s[...] = q_s[...].reshape(BLOCK, 128).T
    gt_s[...] = g_s[...].reshape(BLOCK, 128).T
    lax.fori_loop(0, hi - lo, first_pass, 0)

    total = jnp.sum(total_s[...], axis=0, keepdims=True)
    safe = jnp.logical_and(jnp.max(total) <= 1e30, jnp.min(total) >= 1e-30)

    @pl.when(jnp.logical_not(safe))
    def _():
        m_s[...] = jnp.full_like(m_s, -1e30)

        def highest(t, c):
            raw = mm(k_tile(k_s, t), qt_s[...], NN)
            top = m_s[...]
            for rows in pieces:
                top = jnp.maximum(top, folded(scores(raw, t, rows, masks(t)), jnp.max))
            m_s[...] = top
            return c

        lax.fori_loop(lo, hi, highest, 0)
        top = jnp.max(m_s[...], axis=0, keepdims=True)
        clear()

        def again(t, c):
            weigh(t, masks(t), top)
            return c

        lax.fori_loop(lo, hi, again, 0)

    inv = 1.0 / jnp.sum(total_s[...], axis=0, keepdims=True)
    row_delta = jnp.sum(delta_s[...], axis=0, keepdims=True) * inv

    def store(t, dk, dv):
        at = lax.shift_right_logical(t, 1)
        rows = pl.ds(4 * (t % 2), 4)

        @pl.when(at % 2 == 0)
        def _():
            pair = lax.shift_right_logical(4 - at, 1)
            mine_ref[pair, rows, 0] = dk.reshape(4, 128, 128)
            mine_ref[pair, rows, 1] = dv.reshape(4, 128, 128)

        @pl.when(at % 2 == 1)
        def _():
            pair = lax.shift_right_logical(5 - 2 * core - at, 1)
            send_ref[pair, rows, 0] = dk.reshape(4, 128, 128)
            send_ref[pair, rows, 1] = dv.reshape(4, 128, 128)

    def nothing(t, c):
        zero = jnp.zeros((TILE, 128), jnp.bfloat16)
        store(t, zero, zero)
        return c

    lax.fori_loop(0, lo, nothing, 0)

    def grads(t, c):
        ws, dss = [], []
        for rows in pieces:
            w = s_s[t, rows] * inv
            dss.append((w * (p_s[t, rows] - row_delta)).astype(jnp.bfloat16))
            ws.append(w.astype(jnp.bfloat16))
        w, ds = jnp.concatenate(ws, axis=0), jnp.concatenate(dss, axis=0)
        dv = mm(w, g_s[...].reshape(BLOCK, 128), NN).astype(jnp.bfloat16)
        dk = (mm(ds, q_s[...].reshape(BLOCK, 128), NN) * inv_scale).astype(jnp.bfloat16)
        dq_s[...] += mm(k_tile(k_s, t).T, ds, NN)
        store(t, dk, dv)
        return c

    lax.fori_loop(lo, hi, grads, 0)
    dq_ref[...] = (dq_s[...] * inv_scale).T.astype(jnp.bfloat16).reshape(8, 128, 128)


def attention(doc_lengths, slopes, qg, kvs):
    three = jax.ShapeDtypeStruct((3, 8, 2, 128, 128), jnp.bfloat16)
    smem = pl.BlockSpec(memory_space=pltpu.SMEM)
    anywhere = pl.BlockSpec(memory_space=pl.ANY)
    vmem = pl.BlockSpec(memory_space=pltpu.VMEM)
    return pl.pallas_call(
        attention_kernel,
        out_shape=(jax.ShapeDtypeStruct((8, 128, 128), jnp.bfloat16), three, three),
        in_specs=[smem, smem] + [anywhere] * 7,
        out_specs=(vmem,) * 3,
        scratch_shapes=[
            pltpu.VMEM((8, 128, 128), jnp.bfloat16),
            pltpu.VMEM((8, 128, 128), jnp.bfloat16),
            pltpu.VMEM((40, 128, 128), jnp.bfloat16),
            pltpu.VMEM((40, 128, 128), jnp.bfloat16),
            pltpu.VMEM((128, BLOCK), jnp.bfloat16),
            pltpu.VMEM((128, BLOCK), jnp.bfloat16),
            pltpu.VMEM((TILES, TILE, BLOCK), jnp.float32),
            pltpu.VMEM((TILES, TILE, BLOCK), jnp.float32),
            pltpu.VMEM((8, BLOCK), jnp.float32),
            pltpu.VMEM((8, BLOCK), jnp.float32),
            pltpu.VMEM((8, BLOCK), jnp.float32),
            pltpu.VMEM((128, BLOCK), jnp.float32),
            pltpu.SemaphoreType.DMA((12,)),
        ],
        compiler_params=pltpu.CompilerParams(vmem_limit_bytes=60 * 1024 * 1024),
    )(doc_lengths, slopes, qg, *kvs)


def shifted(x, distance):
    n = lax.axis_size("ctx")
    return lax.ppermute(x, "ctx", [(i, (i + distance) % n) for i in range(n)])


def swapped(x):
    n = lax.axis_size("ctx")
    return lax.ppermute(x, "ctx", [(i, i ^ 1) for i in range(n)])


def to_heads(a, b):
    both = jnp.stack([a.transpose(1, 0, 2), b.transpose(1, 0, 2)], axis=1)
    return lax.all_to_all(both, "head", 0, 0, tiled=True)


def body(queries, keys_in, values, grad_out, slopes, doc_lengths):
    kv = to_heads(keys_in, values)
    qg = to_heads(queries, grad_out)
    one = shifted(kv, 2)
    two = shifted(one, 2)
    dq, mine, send = attention(
        doc_lengths,
        slopes,
        qg,
        (kv, one, two, swapped(kv), swapped(one), swapped(two)),
    )
    total = mine.astype(jnp.float32) + swapped(send).astype(jnp.float32)
    back = shifted(total[2].astype(jnp.bfloat16), -2)
    back = shifted((total[1] + back.astype(jnp.float32)).astype(jnp.bfloat16), -2)
    dkv = total[0] + back.astype(jnp.float32)
    dq = lax.all_to_all(dq, "head", 0, 0, tiled=True)
    dkv = lax.all_to_all(dkv.astype(jnp.bfloat16), "head", 0, 0, tiled=True)
    return (
        dq.transpose(1, 0, 2),
        dkv[:, 0].transpose(1, 0, 2),
        dkv[:, 1].transpose(1, 0, 2),
    )


def solution(mesh):
    placed = P(("ctx", "head"), None, None)
    return jax.shard_map(
        body,
        mesh=mesh,
        in_specs=(placed,) * 4 + (P(), P()),
        out_specs=(placed,) * 3,
        check_vma=False,
    )
```

```python
import math

import jax
import jax.numpy as jnp
from jax import lax
from jax.experimental import pallas as pl
from jax.experimental.pallas import tpu as pltpu
from jax.sharding import PartitionSpec as P

TILE = 512
SHIFT = 9
SUB = 2
DIAG = 8
CHUNK = 128
BLOCK = 1024
SLOTS = 6
TILES = 10
NT = (((1,), (1,)), ((), ()))
NN = (((1,), (0,)), ((), ()))


def mm(a, b, dims):
    return lax.dot_general(a, b, dims, preferred_element_type=jnp.float32)


def attention_kernel(doc_ref, slope_ref, qg, *refs):
    kvs = refs[:SLOTS]
    dq_ref, mine_ref, send_ref = refs[SLOTS : SLOTS + 3]
    q_s, g_s, k_s, v_s, qt_s, gt_s, s_s, p_s, m_s, total_s, delta_s, dq_s, out_s, sems = refs[
        SLOTS + 3 :
    ]
    block = lax.axis_index("ctx")
    core = block % 2
    q0 = block * BLOCK
    base = q0 - 4 * BLOCK
    slope2 = slope_ref[lax.axis_index("head")] * math.log2(math.e)
    inv_scale = 1.0 / math.sqrt(128.0)
    scale2 = inv_scale * math.log2(math.e)

    starts = []
    at = jnp.int32(0)
    for d in range(16):
        starts.append(at)
        at = at + doc_ref[d]

    def start_of(pos):
        found = jnp.zeros_like(pos)
        for s in starts:
            found = jnp.where(pos >= s, s, found)
        return found

    start0, start1 = start_of(q0), start_of(q0 + BLOCK - 1)
    lo = jnp.minimum(lax.shift_right_logical(start0 - base, SHIFT), DIAG)

    def place(slot):
        pair = 2 * (slot % 3)
        return 4 - pair if slot < 3 else 4 - pair + 1 - 2 * core

    def needed(slot):
        at = place(slot)
        return jnp.logical_and(at <= 4, SUB * (at + 1) > lo)

    q_copy = pltpu.make_async_copy(qg.at[:, 0], q_s, sems.at[0])
    g_copy = pltpu.make_async_copy(qg.at[:, 1], g_s, sems.at[1])

    def block_copies(slot, at):
        rows = pl.ds(at * 8, 8)
        return (
            pltpu.make_async_copy(kvs[slot].at[:, 0], k_s.at[rows], sems.at[2 + at]),
            pltpu.make_async_copy(kvs[slot].at[:, 1], v_s.at[rows], sems.at[7 + at]),
        )

    q_copy.start()
    g_copy.start()
    for slot in (0, 3, 1, 4, 2, 5):

        @pl.when(needed(slot))
        def _():
            for copy in block_copies(slot, jnp.clip(place(slot), 0, 4)):
                copy.start()

    def arrived(at):
        for copy in block_copies(0, at):
            copy.wait()

    def leave(at):
        @pl.when(at % 2 == 0)
        def _():
            pair = lax.shift_right_logical(4 - at, 1)
            pltpu.make_async_copy(out_s.at[at], mine_ref.at[pair], sems.at[12 + at]).start()

        @pl.when(at % 2 == 1)
        def _():
            pair = jnp.where(at == 5, 2 * core, lax.shift_right_logical(5 - 2 * core - at, 1))
            pltpu.make_async_copy(out_s.at[at], send_ref.at[pair], sems.at[12 + at]).start()

    def k_tile(ref, t):
        return ref[pl.ds(TILE // 128 * t, TILE // 128)].reshape(TILE, 128)

    row_bias = slope2 * lax.broadcasted_iota(jnp.int32, (TILE, 128), 0).astype(jnp.float32)
    pieces = [slice(i * CHUNK, (i + 1) * CHUNK) for i in range(TILE // CHUNK)]

    def folded(x, reduce):
        return reduce(x.reshape(CHUNK // 8, 8, x.shape[1]), axis=0)

    def masks(t, begin=0):
        k0 = base + t * TILE
        q_pos = q0 + begin + lax.broadcasted_iota(jnp.int32, (1, BLOCK - begin), 1)
        return start_of(q_pos) - k0, q_pos - k0

    def scores(raw, t, rows, limits):
        width = raw.shape[1]
        offset = slope2 * (base + t * TILE - q0 - BLOCK // 2).astype(jnp.float32)
        bias = row_bias[rows] + offset
        s = raw[rows] * scale2 + jnp.concatenate([bias] * (width // 128), axis=1)
        if limits is None:
            return s
        k_pos = lax.broadcasted_iota(jnp.int32, (CHUNK, width), 0) + rows.start
        allowed = jnp.logical_and(k_pos >= limits[0], k_pos <= limits[1])
        return jnp.where(allowed, s, -1e30)

    def weigh(t, limits, top, begin=0):
        cols = slice(begin, BLOCK)
        raw = mm(k_tile(k_s, t), qt_s[:, cols], NN)
        dp = mm(k_tile(v_s, t), gt_s[:, cols], NN)
        total, delta = total_s[:, cols], delta_s[:, cols]
        for rows in pieces:
            s = scores(raw, t, rows, limits)
            p = jnp.exp2(s if top is None else s - top)
            s_s[t, rows, cols] = p
            p_s[t, rows, cols] = dp[rows]
            total = total + folded(p, jnp.sum)
            delta = delta + folded(p * dp[rows], jnp.sum)
        total_s[:, cols] = total
        delta_s[:, cols] = delta

    def clear():
        total_s[...] = jnp.zeros_like(total_s)
        delta_s[...] = jnp.zeros_like(delta_s)

    def first_pass(i, c):
        t = DIAG - 1 - i

        @pl.when(t % SUB == SUB - 1)
        def _():
            arrived(lax.shift_right_logical(t, 10 - SHIFT))

        k0 = base + t * TILE

        @pl.when(k0 >= start1)
        def _():
            weigh(t, None, None)

        @pl.when(k0 < start1)
        def _():
            weigh(t, masks(t), None)

        return c

    def store(t, dk, dv):
        at = lax.shift_right_logical(t, 10 - SHIFT) if not isinstance(t, int) else t // SUB
        rows = pl.ds(TILE // 128 * (t % SUB), TILE // 128)
        out_s[at, rows, 0] = dk.reshape(TILE // 128, 128, 128)
        out_s[at, rows, 1] = dv.reshape(TILE // 128, 128, 128)

    clear()
    dq_s[...] = jnp.zeros_like(dq_s)
    out_s[5] = jnp.zeros((8, 2, 128, 128), jnp.bfloat16)
    leave(jnp.int32(5))

    def nothing(t, c):
        zero = jnp.zeros((TILE, 128), jnp.bfloat16)
        store(t, zero, zero)
        return c

    lax.fori_loop(0, lo, nothing, 0)

    def leave_block(at, c):
        leave(at)
        return c

    lax.fori_loop(0, lax.shift_right_logical(lo, 10 - SHIFT), leave_block, 0)
    q_copy.wait()
    g_copy.wait()
    qt_s[...] = q_s[...].reshape(BLOCK, 128).T
    gt_s[...] = g_s[...].reshape(BLOCK, 128).T
    arrived(4)
    for i in range(SUB):
        weigh(DIAG + i, masks(DIAG + i, i * TILE), None, i * TILE)
    lax.fori_loop(0, DIAG - lo, first_pass, 0)

    total = jnp.sum(total_s[...], axis=0, keepdims=True)
    safe = jnp.logical_and(jnp.max(total) <= 1e30, jnp.min(total) >= 1e-30)

    @pl.when(jnp.logical_not(safe))
    def _():
        m_s[...] = jnp.full_like(m_s, -1e30)

        def highest(t, c):
            raw = mm(k_tile(k_s, t), qt_s[...], NN)
            top = m_s[...]
            for rows in pieces:
                top = jnp.maximum(top, folded(scores(raw, t, rows, masks(t)), jnp.max))
            m_s[...] = top
            return c

        lax.fori_loop(lo, TILES, highest, 0)
        top = jnp.max(m_s[...], axis=0, keepdims=True)
        clear()

        def again(t, c):
            weigh(t, masks(t), top)
            return c

        lax.fori_loop(lo, TILES, again, 0)

    inv = 1.0 / jnp.sum(total_s[...], axis=0, keepdims=True)
    row_delta = jnp.sum(delta_s[...], axis=0, keepdims=True) * inv

    def grads(t, begin=0):
        cols = slice(begin, BLOCK)
        ws, dss = [], []
        for rows in pieces:
            w = s_s[t, rows, cols] * inv[:, cols]
            dss.append((w * (p_s[t, rows, cols] - row_delta[:, cols])).astype(jnp.bfloat16))
            ws.append(w.astype(jnp.bfloat16))
        w, ds = jnp.concatenate(ws, axis=0), jnp.concatenate(dss, axis=0)
        g_t = g_s[begin // 128 :].reshape(BLOCK - begin, 128)
        q_t = q_s[begin // 128 :].reshape(BLOCK - begin, 128)
        dv = mm(w, g_t, NN).astype(jnp.bfloat16)
        dk = (mm(ds, q_t, NN) * inv_scale).astype(jnp.bfloat16)
        dq_s[:, cols] += mm(k_tile(k_s, t).T, ds, NN)
        store(t, dk, dv)

    def second_pass(t, c):
        grads(t)

        @pl.when(t % SUB == SUB - 1)
        def _():
            leave(lax.shift_right_logical(t, 10 - SHIFT))

        return c

    for i in range(SUB):
        grads(DIAG + i, i * TILE)
    leave(jnp.int32(4))
    lax.fori_loop(lo, DIAG, second_pass, 0)
    dq_ref[...] = (dq_s[...] * inv_scale).T.astype(jnp.bfloat16).reshape(8, 128, 128)
    for at in range(6):
        pltpu.make_async_copy(out_s.at[at], mine_ref.at[0], sems.at[12 + at]).wait()


def attention(doc_lengths, slopes, qg, kvs):
    three = jax.ShapeDtypeStruct((3, 8, 2, 128, 128), jnp.bfloat16)
    smem = pl.BlockSpec(memory_space=pltpu.SMEM)
    anywhere = pl.BlockSpec(memory_space=pl.ANY)
    vmem = pl.BlockSpec(memory_space=pltpu.VMEM)
    return pl.pallas_call(
        attention_kernel,
        out_shape=(jax.ShapeDtypeStruct((8, 128, 128), jnp.bfloat16), three, three),
        in_specs=[smem, smem] + [anywhere] * 7,
        out_specs=(vmem, anywhere, anywhere),
        scratch_shapes=[
            pltpu.VMEM((8, 128, 128), jnp.bfloat16),
            pltpu.VMEM((8, 128, 128), jnp.bfloat16),
            pltpu.VMEM((40, 128, 128), jnp.bfloat16),
            pltpu.VMEM((40, 128, 128), jnp.bfloat16),
            pltpu.VMEM((128, BLOCK), jnp.bfloat16),
            pltpu.VMEM((128, BLOCK), jnp.bfloat16),
            pltpu.VMEM((TILES, TILE, BLOCK), jnp.float32),
            pltpu.VMEM((TILES, TILE, BLOCK), jnp.float32),
            pltpu.VMEM((8, BLOCK), jnp.float32),
            pltpu.VMEM((8, BLOCK), jnp.float32),
            pltpu.VMEM((8, BLOCK), jnp.float32),
            pltpu.VMEM((128, BLOCK), jnp.float32),
            pltpu.VMEM((6, 8, 2, 128, 128), jnp.bfloat16),
            pltpu.SemaphoreType.DMA((18,)),
        ],
        compiler_params=pltpu.CompilerParams(vmem_limit_bytes=60 * 1024 * 1024),
    )(doc_lengths, slopes, qg, *kvs)


def shifted(x, distance):
    n = lax.axis_size("ctx")
    return lax.ppermute(x, "ctx", [(i, (i + distance) % n) for i in range(n)])


def swapped(x):
    n = lax.axis_size("ctx")
    return lax.ppermute(x, "ctx", [(i, i ^ 1) for i in range(n)])


def routed(x, target):
    n = lax.axis_size("ctx")
    return lax.ppermute(x, "ctx", [(i, target(i)) for i in range(n)])


def up_the_row(i):
    x, y, core = i // 8, i // 2 % 4, i % 2
    return (x * 4 + (y + 1) % 4) * 2 + core


def up_to_two_before(i):
    x, y, core = i // 8, i // 2 % 4, i % 2
    x = (x - 1) % 4 if y in (1, 2) else x
    return (x * 4 + (y + 1) % 4) * 2 + core


def summed(*parts):
    total = parts[0].astype(jnp.float32)
    for part in parts[1:]:
        total = total + part.astype(jnp.float32)
    return total.astype(jnp.bfloat16)


def to_heads(a, b):
    both = jnp.stack([a.transpose(1, 0, 2), b.transpose(1, 0, 2)], axis=1)
    return lax.all_to_all(both, "head", 0, 0, tiled=True)


def body(queries, keys_in, values, grad_out, slopes, doc_lengths):
    kv = to_heads(keys_in, values)
    qg = to_heads(queries, grad_out)
    one = shifted(kv, 2)
    two = shifted(kv, 4)
    dq, mine, send = attention(
        doc_lengths,
        slopes,
        qg,
        (kv, one, two, swapped(kv), swapped(one), swapped(two)),
    )
    other = swapped(send)
    upper, lower = slice(0, 4), slice(4, 8)
    near = shifted(summed(mine[2, upper], other[2, upper]), -2)
    far = routed(summed(mine[2, lower], other[2, lower]), up_the_row)
    back = jnp.concatenate(
        [
            summed(mine[1, upper], other[1, upper], near),
            summed(mine[1, lower], other[1, lower]),
        ]
    )
    back = shifted(back, -2)
    far = routed(far, up_to_two_before)
    dkv = jnp.concatenate(
        [
            summed(mine[0, upper], other[0, upper], back[upper]),
            summed(mine[0, lower], other[0, lower], back[lower], far),
        ]
    )
    dq = lax.all_to_all(dq, "head", 0, 0, tiled=True)
    dkv = lax.all_to_all(dkv, "head", 0, 0, tiled=True)
    return (
        dq.transpose(1, 0, 2),
        dkv[:, 0].transpose(1, 0, 2),
        dkv[:, 1].transpose(1, 0, 2),
    )


def solution(mesh):
    placed = P(("ctx", "head"), None, None)
    return jax.shard_map(
        body,
        mesh=mesh,
        in_specs=(placed,) * 4 + (P(), P()),
        out_specs=(placed,) * 3,
        check_vma=False,
    )
```

```python
import math

import jax
import jax.numpy as jnp
from jax import lax
from jax.experimental import pallas as pl
from jax.experimental.pallas import tpu as pltpu
from jax.sharding import PartitionSpec as P

TILE = 512
SHIFT = 9
SUB = 2
DIAG = 8
CHUNK = 128
BLOCK = 1024
SLOTS = 6
TILES = 10
NT = (((1,), (1,)), ((), ()))
NN = (((1,), (0,)), ((), ()))


def mm(a, b, dims):
    return lax.dot_general(a, b, dims, preferred_element_type=jnp.float32)


def attention_kernel(doc_ref, slope_ref, qg, *refs):
    kvs = refs[:SLOTS]
    dq_ref, mine_ref, send_ref, far_ref = refs[SLOTS : SLOTS + 4]
    q_s, g_s, k_s, v_s, qt_s, gt_s, s_s, p_s, m_s, total_s, delta_s, dq_s, out_s, sems = refs[
        SLOTS + 4 :
    ]
    block = lax.axis_index("ctx")
    core = block % 2
    q0 = block * BLOCK
    base = q0 - 4 * BLOCK
    slope2 = slope_ref[lax.axis_index("head")] * math.log2(math.e)
    inv_scale = 1.0 / math.sqrt(128.0)
    scale2 = inv_scale * math.log2(math.e)

    starts = []
    at = jnp.int32(0)
    for d in range(16):
        starts.append(at)
        at = at + doc_ref[d]

    def start_of(pos):
        found = jnp.zeros_like(pos)
        for s in starts:
            found = jnp.where(pos >= s, s, found)
        return found

    start0 = start_of(q0)
    lo = jnp.minimum(lax.shift_right_logical(start0 - base, SHIFT), DIAG)

    first_end = q0 + BLOCK
    for s in starts[::-1]:
        first_end = jnp.where(s > q0, jnp.minimum(first_end, s), first_end)
    whole = first_end == q0 + BLOCK
    narrow = first_end <= q0 + BLOCK // 2

    def place(slot):
        pair = 2 * (slot % 3)
        return 4 - pair if slot < 3 else 4 - pair + 1 - 2 * core

    def needed(slot):
        at = place(slot)
        return jnp.logical_and(at <= 4, SUB * (at + 1) > lo)

    q_copy = pltpu.make_async_copy(qg.at[:, 0], q_s, sems.at[0])
    g_copy = pltpu.make_async_copy(qg.at[:, 1], g_s, sems.at[1])

    def block_copies(slot, at):
        rows = pl.ds(at * 8, 8)
        return (
            pltpu.make_async_copy(kvs[slot].at[:, 0], k_s.at[rows], sems.at[2 + at]),
            pltpu.make_async_copy(kvs[slot].at[:, 1], v_s.at[rows], sems.at[7 + at]),
        )

    q_copy.start()
    g_copy.start()
    for slot in (0, 3, 1, 4, 2, 5):

        @pl.when(needed(slot))
        def _():
            for copy in block_copies(slot, jnp.clip(place(slot), 0, 4)):
                copy.start()

    def arrived(at):
        for copy in block_copies(0, at):
            copy.wait()

    def leave(at):
        @pl.when(at % 2 == 0)
        def _():
            pair = lax.shift_right_logical(4 - at, 1)
            pltpu.make_async_copy(out_s.at[at], mine_ref.at[pair], sems.at[12 + at]).start()

        @pl.when(at % 2 == 1)
        def _():
            pair = jnp.where(at == 5, 2 * core, lax.shift_right_logical(5 - 2 * core - at, 1))

            @pl.when(pair < 2)
            def _():
                pltpu.make_async_copy(out_s.at[at], send_ref.at[pair], sems.at[12 + at]).start()

            @pl.when(pair == 2)
            def _():
                pltpu.make_async_copy(out_s.at[at], far_ref, sems.at[12 + at]).start()

    def k_tile(ref, t):
        return ref[pl.ds(TILE // 128 * t, TILE // 128)].reshape(TILE, 128)

    row_bias = slope2 * lax.broadcasted_iota(jnp.int32, (TILE, 128), 0).astype(jnp.float32)
    pieces = [slice(i * CHUNK, (i + 1) * CHUNK) for i in range(TILE // CHUNK)]

    def folded(x, reduce):
        return reduce(x.reshape(CHUNK // 8, 8, x.shape[1]), axis=0)

    def masks(t, begin=0):
        k0 = base + t * TILE
        q_pos = q0 + begin + lax.broadcasted_iota(jnp.int32, (1, BLOCK - begin), 1)
        return start_of(q_pos) - k0, q_pos - k0

    def scores(raw, t, rows, limits):
        width = raw.shape[1]
        offset = slope2 * (base + t * TILE - q0 - BLOCK // 2).astype(jnp.float32)
        bias = row_bias[rows] + offset
        if not isinstance(limits, tuple):
            k_pos = lax.broadcasted_iota(jnp.int32, (CHUNK, 128), 0) + rows.start
            bias = jnp.where(k_pos >= start0 - (base + t * TILE), bias, -1e30)
        s = raw[rows] * scale2 + jnp.concatenate([bias] * (width // 128), axis=1)
        if limits is None:
            return s
        if not isinstance(limits, tuple):
            return s + limits
        k_pos = lax.broadcasted_iota(jnp.int32, (CHUNK, width), 0) + rows.start
        allowed = jnp.logical_and(k_pos >= limits[0], k_pos <= limits[1])
        return jnp.where(allowed, s, -1e30)

    def weigh(t, limits, top, begin=0, end=BLOCK):
        cols = slice(begin, end)
        raw = mm(k_tile(k_s, t), qt_s[:, cols], NN)
        dp = mm(k_tile(v_s, t), gt_s[:, cols], NN)
        total, delta = total_s[:, cols], delta_s[:, cols]
        for rows in pieces:
            s = scores(raw, t, rows, limits)
            p = jnp.exp2(s if top is None else s - top)
            s_s[t, rows, cols] = p
            p_s[t, rows, cols] = dp[rows]
            total = total + folded(p, jnp.sum)
            delta = delta + folded(p * dp[rows], jnp.sum)
        total_s[:, cols] = total
        delta_s[:, cols] = delta

    def clear():
        total_s[...] = jnp.zeros_like(total_s)
        delta_s[...] = jnp.zeros_like(delta_s)

    def shut(width):
        q_pos = q0 + lax.broadcasted_iota(jnp.int32, (1, width), 1)
        return jnp.where(q_pos < first_end, 0.0, -1e30)

    def first_pass(i, c):
        t = DIAG - 1 - i

        @pl.when(t % SUB == SUB - 1)
        def _():
            arrived(lax.shift_right_logical(t, 10 - SHIFT))

        @pl.when(whole)
        def _():
            weigh(t, None, None)

        @pl.when(jnp.logical_not(jnp.logical_or(whole, narrow)))
        def _():
            weigh(t, shut(BLOCK), None)

        @pl.when(narrow)
        def _():
            weigh(t, shut(BLOCK // 2), None, 0, BLOCK // 2)

        return c

    def store(t, dk, dv):
        at = lax.shift_right_logical(t, 10 - SHIFT) if not isinstance(t, int) else t // SUB
        rows = pl.ds(TILE // 128 * (t % SUB), TILE // 128)
        out_s[at, rows, 0] = dk.reshape(TILE // 128, 128, 128)
        out_s[at, rows, 1] = dv.reshape(TILE // 128, 128, 128)

    clear()
    dq_s[...] = jnp.zeros_like(dq_s)
    out_s[5] = jnp.zeros((8, 2, 128, 128), jnp.bfloat16)
    leave(jnp.int32(5))

    def nothing(t, c):
        zero = jnp.zeros((TILE, 128), jnp.bfloat16)
        store(t, zero, zero)
        return c

    lax.fori_loop(0, lo, nothing, 0)

    def leave_block(at, c):
        leave(at)
        return c

    lax.fori_loop(0, lax.shift_right_logical(lo, 10 - SHIFT), leave_block, 0)
    q_copy.wait()
    g_copy.wait()
    qt_s[...] = q_s[...].reshape(BLOCK, 128).T
    gt_s[...] = g_s[...].reshape(BLOCK, 128).T
    arrived(4)
    for i in range(SUB):
        weigh(DIAG + i, masks(DIAG + i, i * TILE), None, i * TILE)
    lax.fori_loop(0, DIAG - lo, first_pass, 0)

    total = jnp.sum(total_s[...], axis=0, keepdims=True)
    safe = jnp.logical_and(jnp.max(total) <= 1e30, jnp.min(total) >= 1e-30)

    @pl.when(jnp.logical_not(safe))
    def _():
        m_s[...] = jnp.full_like(m_s, -1e30)

        def highest(t, c):
            raw = mm(k_tile(k_s, t), qt_s[...], NN)
            top = m_s[...]
            for rows in pieces:
                top = jnp.maximum(top, folded(scores(raw, t, rows, masks(t)), jnp.max))
            m_s[...] = top
            return c

        lax.fori_loop(lo, TILES, highest, 0)
        top = jnp.max(m_s[...], axis=0, keepdims=True)
        clear()

        def again(t, c):
            weigh(t, masks(t), top)
            return c

        lax.fori_loop(lo, TILES, again, 0)

    inv = 1.0 / jnp.sum(total_s[...], axis=0, keepdims=True)
    row_delta = jnp.sum(delta_s[...], axis=0, keepdims=True) * inv

    def grads(t, begin=0, end=BLOCK):
        cols = slice(begin, end)
        ws, dss = [], []
        for rows in pieces:
            w = s_s[t, rows, cols] * inv[:, cols]
            dss.append((w * (p_s[t, rows, cols] - row_delta[:, cols])).astype(jnp.bfloat16))
            ws.append(w.astype(jnp.bfloat16))
        w, ds = jnp.concatenate(ws, axis=0), jnp.concatenate(dss, axis=0)
        g_t = g_s[begin // 128 : end // 128].reshape(end - begin, 128)
        q_t = q_s[begin // 128 : end // 128].reshape(end - begin, 128)
        dv = mm(w, g_t, NN).astype(jnp.bfloat16)
        dk = (mm(ds, q_t, NN) * inv_scale).astype(jnp.bfloat16)
        dq_s[:, cols] += mm(k_tile(k_s, t).T, ds, NN)
        store(t, dk, dv)

    def second_pass(t, c):
        @pl.when(narrow)
        def _():
            grads(t, 0, BLOCK // 2)

        @pl.when(jnp.logical_not(narrow))
        def _():
            grads(t)

        @pl.when(t % SUB == SUB - 1)
        def _():
            leave(lax.shift_right_logical(t, 10 - SHIFT))

        return c

    for i in range(SUB):
        grads(DIAG + i, i * TILE)
    leave(jnp.int32(4))
    lax.fori_loop(lo, DIAG, second_pass, 0)
    dq_ref[...] = (dq_s[...] * inv_scale).T.astype(jnp.bfloat16).reshape(8, 128, 128)
    for at in range(6):
        pltpu.make_async_copy(out_s.at[at], mine_ref.at[0], sems.at[12 + at]).wait()


def attention(doc_lengths, slopes, qg, kvs):
    three = jax.ShapeDtypeStruct((3, 8, 2, 128, 128), jnp.bfloat16)
    two = jax.ShapeDtypeStruct((2, 8, 2, 128, 128), jnp.bfloat16)
    one = jax.ShapeDtypeStruct((8, 2, 128, 128), jnp.bfloat16)
    smem = pl.BlockSpec(memory_space=pltpu.SMEM)
    anywhere = pl.BlockSpec(memory_space=pl.ANY)
    vmem = pl.BlockSpec(memory_space=pltpu.VMEM)
    return pl.pallas_call(
        attention_kernel,
        out_shape=(jax.ShapeDtypeStruct((8, 128, 128), jnp.bfloat16), three, two, one),
        in_specs=[smem, smem] + [anywhere] * 7,
        out_specs=(vmem, anywhere, anywhere, anywhere),
        scratch_shapes=[
            pltpu.VMEM((8, 128, 128), jnp.bfloat16),
            pltpu.VMEM((8, 128, 128), jnp.bfloat16),
            pltpu.VMEM((40, 128, 128), jnp.bfloat16),
            pltpu.VMEM((40, 128, 128), jnp.bfloat16),
            pltpu.VMEM((128, BLOCK), jnp.bfloat16),
            pltpu.VMEM((128, BLOCK), jnp.bfloat16),
            pltpu.VMEM((TILES, TILE, BLOCK), jnp.float32),
            pltpu.VMEM((TILES, TILE, BLOCK), jnp.float32),
            pltpu.VMEM((8, BLOCK), jnp.float32),
            pltpu.VMEM((8, BLOCK), jnp.float32),
            pltpu.VMEM((8, BLOCK), jnp.float32),
            pltpu.VMEM((128, BLOCK), jnp.float32),
            pltpu.VMEM((6, 8, 2, 128, 128), jnp.bfloat16),
            pltpu.SemaphoreType.DMA((18,)),
        ],
        compiler_params=pltpu.CompilerParams(vmem_limit_bytes=60 * 1024 * 1024),
    )(doc_lengths, slopes, qg, *kvs)


def shifted(x, distance):
    n = lax.axis_size("ctx")
    return lax.ppermute(x, "ctx", [(i, (i + distance) % n) for i in range(n)])


def swapped(x):
    n = lax.axis_size("ctx")
    return lax.ppermute(x, "ctx", [(i, i ^ 1) for i in range(n)])


def routed(x, target):
    n = lax.axis_size("ctx")
    return lax.ppermute(x, "ctx", [(i, target(i)) for i in range(n)])


def up_the_row(i):
    x, y, core = i // 8, i // 2 % 4, i % 2
    return (x * 4 + (y + 1) % 4) * 2 + core


def up_to_two_before(i):
    x, y, core = i // 8, i // 2 % 4, i % 2
    x = (x - 1) % 4 if y in (1, 2) else x
    return (x * 4 + (y + 1) % 4) * 2 + core


def padded(x, before, after):
    return lax.pad(x, jnp.zeros((), x.dtype), ((before, after, 0),) + ((0, 0, 0),) * 3)


def summed(*parts):
    total = parts[0].astype(jnp.float32)
    for part in parts[1:]:
        total = total + part.astype(jnp.float32)
    return total.astype(jnp.bfloat16)


def to_heads(a, b):
    both = jnp.stack([a.transpose(1, 0, 2), b.transpose(1, 0, 2)], axis=1)
    return lax.all_to_all(both, "head", 0, 0, tiled=True)


def body(queries, keys_in, values, grad_out, slopes, doc_lengths):
    kv = to_heads(keys_in, values)
    qg = to_heads(queries, grad_out)
    one = shifted(kv, 2)
    two = shifted(kv, 4)
    dq, mine, send, send_far = attention(
        doc_lengths,
        slopes,
        qg,
        (kv, one, two, swapped(kv), swapped(one), swapped(two)),
    )
    far_other = swapped(send_far)
    other = swapped(send)
    upper, lower = slice(0, 4), slice(4, 8)
    near = shifted(summed(mine[2, upper], far_other[upper]), -2)
    far = routed(summed(mine[2, lower], far_other[lower]), up_the_row)
    back = shifted(summed(mine[1], other[1], padded(near, 0, 4)), -2)
    far = routed(far, up_to_two_before)
    dkv = summed(mine[0], other[0], back, padded(far, 4, 0))
    dq = lax.all_to_all(dq, "head", 0, 0, tiled=True)
    dkv = lax.all_to_all(dkv, "head", 0, 0, tiled=True)
    return (
        dq.transpose(1, 0, 2),
        dkv[:, 0].transpose(1, 0, 2),
        dkv[:, 1].transpose(1, 0, 2),
    )


def solution(mesh):
    placed = P(("ctx", "head"), None, None)
    return jax.shard_map(
        body,
        mesh=mesh,
        in_specs=(placed,) * 4 + (P(), P()),
        out_specs=(placed,) * 3,
        check_vma=False,
    )
```

```python
import math

import jax
import jax.numpy as jnp
from jax import lax
from jax.experimental import pallas as pl
from jax.experimental.pallas import tpu as pltpu
from jax.sharding import PartitionSpec as P

TILE = 512
SHIFT = 9
SUB = 2
DIAG = 8
CHUNK = 128
BLOCK = 1024
SLOTS = 6
TILES = 10
NT = (((1,), (1,)), ((), ()))
NN = (((1,), (0,)), ((), ()))


def mm(a, b, dims):
    return lax.dot_general(a, b, dims, preferred_element_type=jnp.float32)


def attention_kernel(doc_ref, slope_ref, qg, *refs):
    own, one, two_up, two_down, own_s, one_s, two_up_s, two_down_s = refs[:8]
    kvs = ((own,), (one,), (two_up, two_down), (own_s,), (one_s,), (two_up_s, two_down_s))
    dq_ref, mine_ref, send_ref, far_ref = refs[8:12]
    q_s, g_s, k_s, v_s, qt_s, gt_s, s_s, p_s, m_s, total_s, delta_s, dq_s, out_s, sems = refs[
        12:
    ]
    block = lax.axis_index("ctx")
    core = block % 2
    q0 = block * BLOCK
    base = q0 - 4 * BLOCK
    slope2 = slope_ref[lax.axis_index("head")] * math.log2(math.e)
    inv_scale = 1.0 / math.sqrt(128.0)
    scale2 = inv_scale * math.log2(math.e)

    starts = []
    at = jnp.int32(0)
    for d in range(16):
        starts.append(at)
        at = at + doc_ref[d]

    def start_of(pos):
        found = jnp.zeros_like(pos)
        for s in starts:
            found = jnp.where(pos >= s, s, found)
        return found

    start0 = start_of(q0)
    lo = jnp.minimum(lax.shift_right_logical(start0 - base, SHIFT), DIAG)

    first_end = q0 + BLOCK
    for s in starts[::-1]:
        first_end = jnp.where(s > q0, jnp.minimum(first_end, s), first_end)
    whole = first_end == q0 + BLOCK
    narrow = first_end <= q0 + BLOCK // 2

    def place(slot):
        pair = 2 * (slot % 3)
        return 4 - pair if slot < 3 else 4 - pair + 1 - 2 * core

    def needed(slot):
        at = place(slot)
        return jnp.logical_and(at <= 4, SUB * (at + 1) > lo)

    q_copy = pltpu.make_async_copy(qg.at[:, 0], q_s, sems.at[0])
    g_copy = pltpu.make_async_copy(qg.at[:, 1], g_s, sems.at[1])

    def start_copies(slot, at):
        rows = 8 // len(kvs[slot])
        for i, kv in enumerate(kvs[slot]):
            place = pl.ds(at * 8 + i * rows, rows)
            pltpu.make_async_copy(kv.at[:, 0], k_s.at[place], sems.at[2 + at]).start()
            pltpu.make_async_copy(kv.at[:, 1], v_s.at[place], sems.at[7 + at]).start()

    q_copy.start()
    g_copy.start()
    for slot in (0, 3, 1, 4, 2, 5):

        @pl.when(needed(slot))
        def _():
            start_copies(slot, jnp.clip(place(slot), 0, 4))

    def arrived(at):
        rows = pl.ds(at * 8, 8)
        pltpu.make_async_copy(own.at[:, 0], k_s.at[rows], sems.at[2 + at]).wait()
        pltpu.make_async_copy(own.at[:, 1], v_s.at[rows], sems.at[7 + at]).wait()

    def leave(at):
        @pl.when(at % 2 == 0)
        def _():
            pair = lax.shift_right_logical(4 - at, 1)
            pltpu.make_async_copy(out_s.at[at], mine_ref.at[pair], sems.at[12 + at]).start()

        @pl.when(at % 2 == 1)
        def _():
            pair = jnp.where(at == 5, 2 * core, lax.shift_right_logical(5 - 2 * core - at, 1))

            @pl.when(pair < 2)
            def _():
                pltpu.make_async_copy(out_s.at[at], send_ref.at[pair], sems.at[12 + at]).start()

            @pl.when(pair == 2)
            def _():
                pltpu.make_async_copy(out_s.at[at], far_ref, sems.at[12 + at]).start()

    def k_tile(ref, t):
        return ref[pl.ds(TILE // 128 * t, TILE // 128)].reshape(TILE, 128)

    row_bias = slope2 * lax.broadcasted_iota(jnp.int32, (TILE, 128), 0).astype(jnp.float32)
    pieces = [slice(i * CHUNK, (i + 1) * CHUNK) for i in range(TILE // CHUNK)]

    def folded(x, reduce):
        return reduce(x.reshape(CHUNK // 8, 8, x.shape[1]), axis=0)

    def masks(t, begin=0):
        k0 = base + t * TILE
        q_pos = q0 + begin + lax.broadcasted_iota(jnp.int32, (1, BLOCK - begin), 1)
        return start_of(q_pos) - k0, q_pos - k0

    def scores(raw, t, rows, limits):
        width = raw.shape[1]
        offset = slope2 * (base + t * TILE - q0 - BLOCK // 2).astype(jnp.float32)
        bias = row_bias[rows] + offset
        if not isinstance(limits, tuple):
            k_pos = lax.broadcasted_iota(jnp.int32, (CHUNK, 128), 0) + rows.start
            bias = jnp.where(k_pos >= start0 - (base + t * TILE), bias, -1e30)
        s = raw[rows] * scale2 + jnp.concatenate([bias] * (width // 128), axis=1)
        if limits is None:
            return s
        if not isinstance(limits, tuple):
            return s + limits
        k_pos = lax.broadcasted_iota(jnp.int32, (CHUNK, width), 0) + rows.start
        allowed = jnp.logical_and(k_pos >= limits[0], k_pos <= limits[1])
        return jnp.where(allowed, s, -1e30)

    def weigh(t, limits, top, begin=0, end=BLOCK):
        cols = slice(begin, end)
        raw = mm(k_tile(k_s, t), qt_s[:, cols], NN)
        dp = mm(k_tile(v_s, t), gt_s[:, cols], NN)
        total, delta = total_s[:, cols], delta_s[:, cols]
        for rows in pieces:
            s = scores(raw, t, rows, limits)
            p = jnp.exp2(s if top is None else s - top)
            s_s[t, rows, cols] = p
            p_s[t, rows, cols] = dp[rows]
            total = total + folded(p, jnp.sum)
            delta = delta + folded(p * dp[rows], jnp.sum)
        total_s[:, cols] = total
        delta_s[:, cols] = delta

    def clear():
        total_s[...] = jnp.zeros_like(total_s)
        delta_s[...] = jnp.zeros_like(delta_s)

    def shut(width):
        q_pos = q0 + lax.broadcasted_iota(jnp.int32, (1, width), 1)
        return jnp.where(q_pos < first_end, 0.0, -1e30)

    def weigh_tiles(tiles):
        @pl.when(whole)
        def _():
            for t in tiles:
                weigh(t, None, None)

        @pl.when(jnp.logical_not(jnp.logical_or(whole, narrow)))
        def _():
            for t in tiles:
                weigh(t, shut(BLOCK), None)

        @pl.when(narrow)
        def _():
            for t in tiles:
                weigh(t, shut(BLOCK // 2), None, 0, BLOCK // 2)

    def first_pass(i, c):
        at = DIAG // SUB - 1 - i
        arrived(at)
        weigh_tiles((SUB * at + 1, SUB * at))
        return c

    def store(t, dk, dv):
        at = lax.shift_right_logical(t, 10 - SHIFT) if not isinstance(t, int) else t // SUB
        rows = pl.ds(TILE // 128 * (t % SUB), TILE // 128)
        out_s[at, rows, 0] = dk.reshape(TILE // 128, 128, 128)
        out_s[at, rows, 1] = dv.reshape(TILE // 128, 128, 128)

    clear()
    dq_s[...] = jnp.zeros_like(dq_s)
    out_s[5] = jnp.zeros((8, 2, 128, 128), jnp.bfloat16)
    leave(jnp.int32(5))

    def nothing(t, c):
        zero = jnp.zeros((TILE, 128), jnp.bfloat16)
        store(t, zero, zero)
        return c

    lax.fori_loop(0, lo, nothing, 0)

    def leave_block(at, c):
        leave(at)
        return c

    lax.fori_loop(0, lax.shift_right_logical(lo, 10 - SHIFT), leave_block, 0)
    q_copy.wait()
    g_copy.wait()
    qt_s[...] = q_s[...].reshape(BLOCK, 128).T
    gt_s[...] = g_s[...].reshape(BLOCK, 128).T
    arrived(4)
    for i in range(SUB):
        weigh(DIAG + i, masks(DIAG + i, i * TILE), None, i * TILE)
    whole_blocks = lax.shift_right_logical(DIAG - lo, 10 - SHIFT)
    lax.fori_loop(0, whole_blocks, first_pass, 0)

    @pl.when(lo % SUB == 1)
    def _():
        arrived(lax.shift_right_logical(lo, 10 - SHIFT))
        weigh_tiles((lo,))


    total = jnp.sum(total_s[...], axis=0, keepdims=True)
    safe = jnp.logical_and(jnp.max(total) <= 1e30, jnp.min(total) >= 1e-30)

    @pl.when(jnp.logical_not(safe))
    def _():
        m_s[...] = jnp.full_like(m_s, -1e30)

        def highest(t, c):
            raw = mm(k_tile(k_s, t), qt_s[...], NN)
            top = m_s[...]
            for rows in pieces:
                top = jnp.maximum(top, folded(scores(raw, t, rows, masks(t)), jnp.max))
            m_s[...] = top
            return c

        lax.fori_loop(lo, TILES, highest, 0)
        top = jnp.max(m_s[...], axis=0, keepdims=True)
        clear()

        def again(t, c):
            weigh(t, masks(t), top)
            return c

        lax.fori_loop(lo, TILES, again, 0)

    inv = 1.0 / jnp.sum(total_s[...], axis=0, keepdims=True)
    row_delta = jnp.sum(delta_s[...], axis=0, keepdims=True) * inv

    def grads(t, begin=0, end=BLOCK):
        cols = slice(begin, end)
        ws, dss = [], []
        for rows in pieces:
            w = s_s[t, rows, cols] * inv[:, cols]
            dss.append((w * (p_s[t, rows, cols] - row_delta[:, cols])).astype(jnp.bfloat16))
            ws.append(w.astype(jnp.bfloat16))
        w, ds = jnp.concatenate(ws, axis=0), jnp.concatenate(dss, axis=0)
        g_t = g_s[begin // 128 : end // 128].reshape(end - begin, 128)
        q_t = q_s[begin // 128 : end // 128].reshape(end - begin, 128)
        dv = mm(w, g_t, NN).astype(jnp.bfloat16)
        dk = (mm(ds, q_t, NN) * inv_scale).astype(jnp.bfloat16)
        dq_s[:, cols] += mm(k_tile(k_s, t).T, ds, NN)
        store(t, dk, dv)

    def grads_tiles(tiles, at):
        @pl.when(narrow)
        def _():
            for t in tiles:
                grads(t, 0, BLOCK // 2)

        @pl.when(jnp.logical_not(narrow))
        def _():
            for t in tiles:
                grads(t)

        leave(at)

    def second_pass(i, c):
        at = DIAG // SUB - 1 - i
        grads_tiles((SUB * at, SUB * at + 1), at)
        return c

    for i in range(SUB):
        grads(DIAG + i, i * TILE)
    leave(jnp.int32(4))
    lax.fori_loop(0, whole_blocks, second_pass, 0)

    @pl.when(lo % SUB == 1)
    def _():
        grads_tiles((lo,), lax.shift_right_logical(lo, 10 - SHIFT))

    dq_ref[...] = (dq_s[...] * inv_scale).T.astype(jnp.bfloat16).reshape(8, 128, 128)
    for at in range(6):
        pltpu.make_async_copy(out_s.at[at], mine_ref.at[0], sems.at[12 + at]).wait()


def attention(doc_lengths, slopes, qg, kvs):
    three = jax.ShapeDtypeStruct((3, 8, 2, 128, 128), jnp.bfloat16)
    two = jax.ShapeDtypeStruct((2, 8, 2, 128, 128), jnp.bfloat16)
    one = jax.ShapeDtypeStruct((8, 2, 128, 128), jnp.bfloat16)
    smem = pl.BlockSpec(memory_space=pltpu.SMEM)
    anywhere = pl.BlockSpec(memory_space=pl.ANY)
    vmem = pl.BlockSpec(memory_space=pltpu.VMEM)
    return pl.pallas_call(
        attention_kernel,
        out_shape=(jax.ShapeDtypeStruct((8, 128, 128), jnp.bfloat16), three, two, one),
        in_specs=[smem, smem] + [anywhere] * 9,
        out_specs=(vmem, anywhere, anywhere, anywhere),
        scratch_shapes=[
            pltpu.VMEM((8, 128, 128), jnp.bfloat16),
            pltpu.VMEM((8, 128, 128), jnp.bfloat16),
            pltpu.VMEM((40, 128, 128), jnp.bfloat16),
            pltpu.VMEM((40, 128, 128), jnp.bfloat16),
            pltpu.VMEM((128, BLOCK), jnp.bfloat16),
            pltpu.VMEM((128, BLOCK), jnp.bfloat16),
            pltpu.VMEM((TILES, TILE, BLOCK), jnp.float32),
            pltpu.VMEM((TILES, TILE, BLOCK), jnp.float32),
            pltpu.VMEM((8, BLOCK), jnp.float32),
            pltpu.VMEM((8, BLOCK), jnp.float32),
            pltpu.VMEM((8, BLOCK), jnp.float32),
            pltpu.VMEM((128, BLOCK), jnp.float32),
            pltpu.VMEM((6, 8, 2, 128, 128), jnp.bfloat16),
            pltpu.SemaphoreType.DMA((18,)),
        ],
        compiler_params=pltpu.CompilerParams(vmem_limit_bytes=60 * 1024 * 1024),
    )(doc_lengths, slopes, qg, *kvs)


def shifted(x, distance):
    n = lax.axis_size("ctx")
    return lax.ppermute(x, "ctx", [(i, (i + distance) % n) for i in range(n)])


def swapped(x):
    n = lax.axis_size("ctx")
    return lax.ppermute(x, "ctx", [(i, i ^ 1) for i in range(n)])


def routed(x, target):
    n = lax.axis_size("ctx")
    return lax.ppermute(x, "ctx", [(i, target(i)) for i in range(n)])


def up_the_row(i):
    x, y, core = i // 8, i // 2 % 4, i % 2
    return (x * 4 + (y + 1) % 4) * 2 + core


def up_to_two_before(i):
    x, y, core = i // 8, i // 2 % 4, i % 2
    x = (x - 1) % 4 if y in (1, 2) else x
    return (x * 4 + (y + 1) % 4) * 2 + core


def padded(x, before, after):
    return lax.pad(x, jnp.zeros((), x.dtype), ((before, after, 0),) + ((0, 0, 0),) * 3)


def down_the_row(i):
    x, y, core = i // 8, i // 2 % 4, i % 2
    return (x * 4 + (y - 1) % 4) * 2 + core


def down_to_two_after(i):
    x, y, core = i // 8, i // 2 % 4, i % 2
    x = (x + 1) % 4 if y in (1, 2) else x
    return (x * 4 + (y - 1) % 4) * 2 + core


def summed(*parts):
    total = parts[0].astype(jnp.float32)
    for part in parts[1:]:
        total = total + part.astype(jnp.float32)
    return total.astype(jnp.bfloat16)


def to_heads(a, b):
    both = jnp.stack([a.transpose(1, 0, 2), b.transpose(1, 0, 2)], axis=1)
    return lax.all_to_all(both, "head", 0, 0, tiled=True)


def body(queries, keys_in, values, grad_out, slopes, doc_lengths):
    kv = to_heads(keys_in, values)
    qg = to_heads(queries, grad_out)
    one = shifted(kv, 2)
    two_up = shifted(one[:4], 2)
    two_down = routed(routed(kv[4:], down_the_row), down_to_two_after)
    dq, mine, send, send_far = attention(
        doc_lengths,
        slopes,
        qg,
        (kv, one, two_up, two_down)
        + (swapped(kv), swapped(one), swapped(two_up), swapped(two_down)),
    )
    far_other = swapped(send_far)
    send, far_other = lax.optimization_barrier((send, far_other))
    other = swapped(send)
    upper, lower = slice(0, 4), slice(4, 8)
    near = shifted(summed(mine[2, upper], far_other[upper]), -2)
    far = routed(summed(mine[2, lower], far_other[lower]), up_the_row)
    back = shifted(summed(mine[1], other[1], padded(near, 0, 4)), -2)
    far = routed(far, up_to_two_before)
    dkv = summed(mine[0], other[0], back, padded(far, 4, 0))
    dq = lax.all_to_all(dq, "head", 0, 0, tiled=True)
    dkv = lax.all_to_all(dkv, "head", 0, 0, tiled=True)
    return (
        dq.transpose(1, 0, 2),
        dkv[:, 0].transpose(1, 0, 2),
        dkv[:, 1].transpose(1, 0, 2),
    )


def solution(mesh):
    placed = P(("ctx", "head"), None, None)
    return jax.shard_map(
        body,
        mesh=mesh,
        in_specs=(placed,) * 4 + (P(), P()),
        out_specs=(placed,) * 3,
        check_vma=False,
    )
```

```python
import math

import jax
import jax.numpy as jnp
from jax import lax
from jax.experimental import pallas as pl
from jax.experimental.pallas import tpu as pltpu
from jax.sharding import PartitionSpec as P

TILE = 512
SHIFT = 9
SUB = 2
DIAG = 8
CHUNK = 128
BLOCK = 1024
SLOTS = 6
TILES = 10
NT = (((1,), (1,)), ((), ()))
NN = (((1,), (0,)), ((), ()))


def mm(a, b, dims):
    return lax.dot_general(a, b, dims, preferred_element_type=jnp.float32)


def attention_kernel(doc_ref, slope_ref, qg, *refs):
    own, one, two_up, two_down, own_s, one_s, two_up_s, two_down_s = refs[:8]
    kvs = ((own,), (one,), (two_up, two_down), (own_s,), (one_s,), (two_up_s, two_down_s))
    dq_ref = refs[8]
    mine_refs, send_refs = refs[9:12], refs[12:15]
    q_s, g_s, k_s, v_s, qt_s, gt_s, s_s, p_s, m_s, total_s, delta_s, dq_s, out_s, sems = refs[
        15:
    ]
    block = lax.axis_index("ctx")
    core = block % 2
    q0 = block * BLOCK
    base = q0 - 4 * BLOCK
    slope2 = slope_ref[lax.axis_index("head")] * math.log2(math.e)
    inv_scale = 1.0 / math.sqrt(128.0)
    scale2 = inv_scale * math.log2(math.e)

    starts = []
    at = jnp.int32(0)
    for d in range(16):
        starts.append(at)
        at = at + doc_ref[d]

    def start_of(pos):
        found = jnp.zeros_like(pos)
        for s in starts:
            found = jnp.where(pos >= s, s, found)
        return found

    start0 = start_of(q0)
    lo = jnp.minimum(lax.shift_right_logical(start0 - base, SHIFT), DIAG)

    first_end = q0 + BLOCK
    for s in starts[::-1]:
        first_end = jnp.where(s > q0, jnp.minimum(first_end, s), first_end)
    whole = first_end == q0 + BLOCK
    narrow = first_end <= q0 + BLOCK // 2

    def place(slot):
        pair = 2 * (slot % 3)
        return 4 - pair if slot < 3 else 4 - pair + 1 - 2 * core

    def needed(slot):
        at = place(slot)
        return jnp.logical_and(at <= 4, SUB * (at + 1) > lo)

    q_copy = pltpu.make_async_copy(qg.at[:, 0], q_s, sems.at[0])
    g_copy = pltpu.make_async_copy(qg.at[:, 1], g_s, sems.at[1])

    def start_copies(slot, at):
        rows = 8 // len(kvs[slot])
        for i, kv in enumerate(kvs[slot]):
            place = pl.ds(at * 8 + i * rows, rows)
            pltpu.make_async_copy(kv.at[:, 0], k_s.at[place], sems.at[2 + at]).start()
            pltpu.make_async_copy(kv.at[:, 1], v_s.at[place], sems.at[7 + at]).start()

    q_copy.start()
    g_copy.start()
    for slot in (0, 3, 1, 4, 2, 5):

        @pl.when(needed(slot))
        def _():
            start_copies(slot, jnp.clip(place(slot), 0, 4))

    def arrived(at):
        rows = pl.ds(at * 8, 8)
        pltpu.make_async_copy(own.at[:, 0], k_s.at[rows], sems.at[2 + at]).wait()
        pltpu.make_async_copy(own.at[:, 1], v_s.at[rows], sems.at[7 + at]).wait()

    def leave(at):
        even = at % 2 == 0
        pair = jnp.where(
            even,
            lax.shift_right_logical(jnp.maximum(4 - at, 0), 1),
            jnp.where(
                at == 5, 2 * core, lax.shift_right_logical(jnp.maximum(5 - 2 * core - at, 0), 1)
            ),
        )
        for i in range(3):
            for mine, refs in ((True, mine_refs), (False, send_refs)):

                @pl.when(jnp.logical_and(even == mine, pair == i))
                def _():
                    pltpu.make_async_copy(out_s.at[at], refs[i], sems.at[12 + at]).start()

    def k_tile(ref, t):
        return ref[pl.ds(TILE // 128 * t, TILE // 128)].reshape(TILE, 128)

    row_bias = slope2 * lax.broadcasted_iota(jnp.int32, (TILE, 128), 0).astype(jnp.float32)
    pieces = [slice(i * CHUNK, (i + 1) * CHUNK) for i in range(TILE // CHUNK)]

    def folded(x, reduce):
        return reduce(x.reshape(CHUNK // 8, 8, x.shape[1]), axis=0)

    def kept(t):
        if isinstance(t, int):
            return t - 1
        return jnp.where(t == 0, TILES - 2, t - 1)

    def masks(t, begin=0, end=BLOCK):
        k0 = base + t * TILE
        q_pos = q0 + begin + lax.broadcasted_iota(jnp.int32, (1, end - begin), 1)
        return start_of(q_pos) - k0, q_pos - k0

    def scores(raw, t, rows, limits):
        width = raw.shape[1]
        offset = slope2 * (base + t * TILE - q0 - BLOCK // 2).astype(jnp.float32)
        bias = row_bias[rows] + offset
        if not isinstance(limits, tuple):
            k_pos = lax.broadcasted_iota(jnp.int32, (CHUNK, 128), 0) + rows.start
            bias = jnp.where(k_pos >= start0 - (base + t * TILE), bias, -1e30)
        s = raw[rows] * scale2 + jnp.concatenate([bias] * (width // 128), axis=1)
        if limits is None:
            return s
        if not isinstance(limits, tuple):
            return s + limits
        k_pos = lax.broadcasted_iota(jnp.int32, (CHUNK, width), 0) + rows.start
        allowed = jnp.logical_and(k_pos >= limits[0], k_pos <= limits[1])
        return jnp.where(allowed, s, -1e30)

    def weigh(t, limits, top, begin=0, end=BLOCK):
        cols = slice(begin, end)
        raw = mm(k_tile(k_s, t), qt_s[:, cols], NN)
        dp = mm(k_tile(v_s, t), gt_s[:, cols], NN)
        total, delta = total_s[:, cols], delta_s[:, cols]
        for rows in pieces:
            s = scores(raw, t, rows, limits)
            p = jnp.exp2(s if top is None else s - top)
            s_s[kept(t), rows, cols] = p.astype(jnp.bfloat16)
            p_s[kept(t), rows, cols] = dp[rows]
            total = total + folded(p, jnp.sum)
            delta = delta + folded(p * dp[rows], jnp.sum)
        total_s[:, cols] = total
        delta_s[:, cols] = delta

    def clear():
        total_s[...] = jnp.zeros_like(total_s)
        delta_s[...] = jnp.zeros_like(delta_s)

    def shut(width):
        q_pos = q0 + lax.broadcasted_iota(jnp.int32, (1, width), 1)
        return jnp.where(q_pos < first_end, 0.0, -1e30)

    def weigh_tiles(tiles):
        @pl.when(whole)
        def _():
            for t in tiles:
                weigh(t, None, None)

        @pl.when(jnp.logical_not(jnp.logical_or(whole, narrow)))
        def _():
            for t in tiles:
                weigh(t, shut(BLOCK), None)

        @pl.when(narrow)
        def _():
            for t in tiles:
                weigh(t, shut(BLOCK // 2), None, 0, BLOCK // 2)

    def first_pass(i, c):
        at = DIAG // SUB - 1 - i
        arrived(at)
        weigh_tiles((SUB * at + 1, SUB * at))
        return c

    def store(t, dk, dv):
        at = lax.shift_right_logical(t, 10 - SHIFT) if not isinstance(t, int) else t // SUB
        rows = pl.ds(TILE // 128 * (t % SUB), TILE // 128)
        out_s[at, rows, 0] = dk.reshape(TILE // 128, 128, 128)
        out_s[at, rows, 1] = dv.reshape(TILE // 128, 128, 128)

    clear()
    dq_s[...] = jnp.zeros_like(dq_s)
    out_s[5] = jnp.zeros((8, 2, 128, 128), jnp.bfloat16)
    leave(jnp.int32(5))

    def nothing(t, c):
        zero = jnp.zeros((TILE, 128), jnp.bfloat16)
        store(t, zero, zero)
        return c

    lax.fori_loop(0, lo, nothing, 0)

    def leave_block(at, c):
        leave(at)
        return c

    lax.fori_loop(0, lax.shift_right_logical(lo, 10 - SHIFT), leave_block, 0)
    q_copy.wait()
    g_copy.wait()
    qt_s[...] = q_s[...].reshape(BLOCK, 128).T
    gt_s[...] = g_s[...].reshape(BLOCK, 128).T
    arrived(4)
    for i in range(SUB):
        weigh(DIAG + i, masks(DIAG + i, i * TILE), None, i * TILE)
    whole_blocks = lax.shift_right_logical(DIAG - lo, 10 - SHIFT)
    lax.fori_loop(0, whole_blocks, first_pass, 0)

    @pl.when(lo % SUB == 1)
    def _():
        arrived(lax.shift_right_logical(lo, 10 - SHIFT))
        weigh_tiles((lo,))


    total = jnp.sum(total_s[...], axis=0, keepdims=True)
    safe = jnp.logical_and(jnp.max(total) <= 1e30, jnp.min(total) >= 1e-30)

    @pl.when(jnp.logical_not(safe))
    def _():
        m_s[...] = jnp.full_like(m_s, -1e30)

        def highest(t, c):
            raw = mm(k_tile(k_s, t), qt_s[...], NN)
            top = m_s[...]
            for rows in pieces:
                top = jnp.maximum(top, folded(scores(raw, t, rows, masks(t)), jnp.max))
            m_s[...] = top
            return c

        lax.fori_loop(lo, TILES, highest, 0)
        top = jnp.max(m_s[...], axis=0, keepdims=True)
        clear()

        def again(t, c):
            @pl.when(narrow)
            def _():
                half = BLOCK // 2
                weigh(t, masks(t, 0, half), top[:, :half], 0, half)

            @pl.when(jnp.logical_not(narrow))
            def _():
                weigh(t, masks(t), top)

            return c

        lax.fori_loop(lo, DIAG, again, 0)
        for i in range(SUB):
            begin = i * TILE
            weigh(DIAG + i, masks(DIAG + i, begin), top[:, begin:], begin)

    inv = 1.0 / jnp.sum(total_s[...], axis=0, keepdims=True)
    row_delta = jnp.sum(delta_s[...], axis=0, keepdims=True) * inv

    def grads(t, begin=0, end=BLOCK):
        cols = slice(begin, end)
        ws, dss = [], []
        for rows in pieces:
            w = s_s[kept(t), rows, cols].astype(jnp.float32) * inv[:, cols]
            dss.append((w * (p_s[kept(t), rows, cols] - row_delta[:, cols])).astype(jnp.bfloat16))
            ws.append(w.astype(jnp.bfloat16))
        w, ds = jnp.concatenate(ws, axis=0), jnp.concatenate(dss, axis=0)
        g_t = g_s[begin // 128 : end // 128].reshape(end - begin, 128)
        q_t = q_s[begin // 128 : end // 128].reshape(end - begin, 128)
        dv = mm(w, g_t, NN).astype(jnp.bfloat16)
        dk = (mm(ds, q_t, NN) * inv_scale).astype(jnp.bfloat16)
        dq_s[:, cols] += mm(k_tile(k_s, t).T, ds, NN)
        store(t, dk, dv)

    def grads_tiles(tiles, at):
        @pl.when(narrow)
        def _():
            for t in tiles:
                grads(t, 0, BLOCK // 2)

        @pl.when(jnp.logical_not(narrow))
        def _():
            for t in tiles:
                grads(t)

        leave(at)

    def second_pass(i, c):
        at = DIAG // SUB - 1 - i
        grads_tiles((SUB * at, SUB * at + 1), at)
        return c

    for i in range(SUB):
        grads(DIAG + i, i * TILE)
    leave(jnp.int32(4))
    lax.fori_loop(0, whole_blocks, second_pass, 0)

    @pl.when(lo % SUB == 1)
    def _():
        grads_tiles((lo,), lax.shift_right_logical(lo, 10 - SHIFT))

    dq_ref[...] = (dq_s[...] * inv_scale).T.astype(jnp.bfloat16).reshape(8, 128, 128)
    for at in range(6):
        pltpu.make_async_copy(out_s.at[at], mine_refs[0], sems.at[12 + at]).wait()


def attention(doc_lengths, slopes, qg, kvs):
    one = jax.ShapeDtypeStruct((8, 2, 128, 128), jnp.bfloat16)
    smem = pl.BlockSpec(memory_space=pltpu.SMEM)
    anywhere = pl.BlockSpec(memory_space=pl.ANY)
    vmem = pl.BlockSpec(memory_space=pltpu.VMEM)
    return pl.pallas_call(
        attention_kernel,
        out_shape=(jax.ShapeDtypeStruct((8, 128, 128), jnp.bfloat16),) + (one,) * 6,
        in_specs=[smem, smem] + [anywhere] * 9,
        out_specs=(vmem,) + (anywhere,) * 6,
        scratch_shapes=[
            pltpu.VMEM((8, 128, 128), jnp.bfloat16),
            pltpu.VMEM((8, 128, 128), jnp.bfloat16),
            pltpu.VMEM((40, 128, 128), jnp.bfloat16),
            pltpu.VMEM((40, 128, 128), jnp.bfloat16),
            pltpu.VMEM((128, BLOCK), jnp.bfloat16),
            pltpu.VMEM((128, BLOCK), jnp.bfloat16),
            pltpu.VMEM((TILES - 1, TILE, BLOCK), jnp.bfloat16),
            pltpu.VMEM((TILES - 1, TILE, BLOCK), jnp.float32),
            pltpu.VMEM((8, BLOCK), jnp.float32),
            pltpu.VMEM((8, BLOCK), jnp.float32),
            pltpu.VMEM((8, BLOCK), jnp.float32),
            pltpu.VMEM((128, BLOCK), jnp.float32),
            pltpu.VMEM((6, 8, 2, 128, 128), jnp.bfloat16),
            pltpu.SemaphoreType.DMA((18,)),
        ],
        compiler_params=pltpu.CompilerParams(vmem_limit_bytes=45 * 1024 * 1024),
    )(doc_lengths, slopes, qg, *kvs)


def shifted(x, distance):
    n = lax.axis_size("ctx")
    return lax.ppermute(x, "ctx", [(i, (i + distance) % n) for i in range(n)])


def swapped(x):
    n = lax.axis_size("ctx")
    return lax.ppermute(x, "ctx", [(i, i ^ 1) for i in range(n)])


def routed(x, target):
    n = lax.axis_size("ctx")
    return lax.ppermute(x, "ctx", [(i, target(i)) for i in range(n)])


def up_the_row(i):
    x, y, core = i // 8, i // 2 % 4, i % 2
    return (x * 4 + (y + 1) % 4) * 2 + core


def up_to_two_before(i):
    x, y, core = i // 8, i // 2 % 4, i % 2
    x = (x - 1) % 4 if y in (1, 2) else x
    return (x * 4 + (y + 1) % 4) * 2 + core


def padded(x, before, after):
    return lax.pad(x, jnp.zeros((), x.dtype), ((before, after, 0),) + ((0, 0, 0),) * 3)


def down_the_row(i):
    x, y, core = i // 8, i // 2 % 4, i % 2
    return (x * 4 + (y - 1) % 4) * 2 + core


def down_to_two_after(i):
    x, y, core = i // 8, i // 2 % 4, i % 2
    x = (x + 1) % 4 if y in (1, 2) else x
    return (x * 4 + (y - 1) % 4) * 2 + core


def summed(*parts):
    total = parts[0].astype(jnp.float32)
    for part in parts[1:]:
        total = total + part.astype(jnp.float32)
    return total.astype(jnp.bfloat16)


def to_heads(a, b):
    both = jnp.stack([a.transpose(1, 0, 2), b.transpose(1, 0, 2)], axis=1)
    return lax.all_to_all(both, "head", 0, 0, tiled=True)


def body(queries, keys_in, values, grad_out, slopes, doc_lengths):
    kv = to_heads(keys_in, values)
    qg = to_heads(queries, grad_out)
    one = shifted(kv, 2)
    two_up = shifted(one[:4], 2)
    two_down = routed(routed(kv[4:], down_the_row), down_to_two_after)
    dq, mine, mine_one, mine_two, send, send_one, send_two = attention(
        doc_lengths,
        slopes,
        qg,
        (kv, one, two_up, two_down)
        + (swapped(kv), swapped(one), swapped(two_up), swapped(two_down)),
    )
    other_two = swapped(send_two)
    send_one, send, other_two = lax.optimization_barrier((send_one, send, other_two))
    other_one = swapped(send_one)
    other = swapped(send)
    upper, lower = slice(0, 4), slice(4, 8)
    near = shifted(summed(mine_two[upper], other_two[upper]), -2)
    far = routed(summed(mine_two[lower], other_two[lower]), up_the_row)
    back = shifted(summed(mine_one, other_one, padded(near, 0, 4)), -2)
    far = routed(far, up_to_two_before)
    dkv = summed(mine, other, padded(far, 4, 0))
    dkv, back = lax.optimization_barrier((dkv, back))
    dkv = summed(dkv, back)
    dq = lax.all_to_all(dq, "head", 0, 0, tiled=True)
    dkv = lax.all_to_all(dkv, "head", 0, 0, tiled=True)
    return (
        dq.transpose(1, 0, 2),
        dkv[:, 0].transpose(1, 0, 2),
        dkv[:, 1].transpose(1, 0, 2),
    )


def solution(mesh):
    placed = P(("ctx", "head"), None, None)
    return jax.shard_map(
        body,
        mesh=mesh,
        in_specs=(placed,) * 4 + (P(), P()),
        out_specs=(placed,) * 3,
        check_vma=False,
    )
```

```python
import math

import jax
import jax.numpy as jnp
from jax import lax
from jax.experimental import pallas as pl
from jax.experimental.pallas import tpu as pltpu
from jax.sharding import PartitionSpec as P

TILE = 512
SHIFT = 9
SUB = 2
DIAG = 8
CHUNK = 128
BLOCK = 1024
SLOTS = 6
TILES = 10
NT = (((1,), (1,)), ((), ()))
NN = (((1,), (0,)), ((), ()))


def mm(a, b, dims):
    return lax.dot_general(a, b, dims, preferred_element_type=jnp.float32)


def attention_kernel(doc_ref, slope_ref, qg, *refs):
    own, one, two_up, two_down, own_s, one_s, two_up_s, two_down_s = refs[:8]
    kvs = ((own,), (one,), (two_up, two_down), (own_s,), (one_s,), (two_up_s, two_down_s))
    dq_ref = refs[8]
    mine_refs, send_refs = refs[9:12], refs[12:15]
    q_s, g_s, k_s, v_s, qt_s, gt_s, s_s, p_s, m_s, total_s, delta_s, dq_s, out_s, sems = refs[
        15:
    ]
    block = lax.axis_index("ctx")
    core = block % 2
    q0 = block * BLOCK
    base = q0 - 4 * BLOCK
    slope2 = slope_ref[lax.axis_index("head")] * math.log2(math.e)
    inv_scale = 1.0 / math.sqrt(128.0)
    scale2 = inv_scale * math.log2(math.e)

    starts = []
    at = jnp.int32(0)
    for d in range(16):
        starts.append(at)
        at = at + doc_ref[d]

    def start_of(pos):
        found = jnp.zeros_like(pos)
        for s in starts:
            found = jnp.where(pos >= s, s, found)
        return found

    start0 = start_of(q0)
    lo = jnp.minimum(lax.shift_right_logical(start0 - base, SHIFT), DIAG)

    first_end = q0 + BLOCK
    for s in starts[::-1]:
        first_end = jnp.where(s > q0, jnp.minimum(first_end, s), first_end)
    whole = first_end == q0 + BLOCK
    narrow = first_end <= q0 + BLOCK // 2

    def place(slot):
        pair = 2 * (slot % 3)
        return 4 - pair if slot < 3 else 4 - pair + 1 - 2 * core

    def needed(slot):
        at = place(slot)
        return jnp.logical_and(at <= 4, SUB * (at + 1) > lo)

    q_copy = pltpu.make_async_copy(qg.at[:, 0], q_s, sems.at[0])
    g_copy = pltpu.make_async_copy(qg.at[:, 1], g_s, sems.at[1])

    def start_copies(slot, at):
        rows = 8 // len(kvs[slot])
        for i, kv in enumerate(kvs[slot]):
            place = pl.ds(at * 8 + i * rows, rows)
            pltpu.make_async_copy(kv.at[:, 0], k_s.at[place], sems.at[2 + at]).start()
            pltpu.make_async_copy(kv.at[:, 1], v_s.at[place], sems.at[7 + at]).start()

    q_copy.start()
    g_copy.start()
    for slot in (0, 3, 1, 4, 2, 5):

        @pl.when(needed(slot))
        def _():
            start_copies(slot, jnp.clip(place(slot), 0, 4))

    def arrived(at):
        rows = pl.ds(at * 8, 8)
        pltpu.make_async_copy(own.at[:, 0], k_s.at[rows], sems.at[2 + at]).wait()
        pltpu.make_async_copy(own.at[:, 1], v_s.at[rows], sems.at[7 + at]).wait()

    def leave(at):
        even = at % 2 == 0
        pair = jnp.where(
            even,
            lax.shift_right_logical(jnp.maximum(4 - at, 0), 1),
            jnp.where(
                at == 5, 2 * core, lax.shift_right_logical(jnp.maximum(5 - 2 * core - at, 0), 1)
            ),
        )
        for i in range(3):
            for mine, refs in ((True, mine_refs), (False, send_refs)):

                @pl.when(jnp.logical_and(even == mine, pair == i))
                def _():
                    pltpu.make_async_copy(out_s.at[at], refs[i], sems.at[12 + at]).start()

    def k_tile(ref, t):
        return ref[pl.ds(TILE // 128 * t, TILE // 128)].reshape(TILE, 128)

    row_bias = slope2 * lax.broadcasted_iota(jnp.int32, (TILE, 128), 0).astype(jnp.float32)
    pieces = [slice(i * CHUNK, (i + 1) * CHUNK) for i in range(TILE // CHUNK)]

    def folded(x, reduce):
        return reduce(x.reshape(CHUNK // 8, 8, x.shape[1]), axis=0)

    def kept(t):
        if isinstance(t, int):
            return t - 1
        return jnp.where(t == 0, TILES - 2, t - 1)

    def masks(t, begin=0, end=BLOCK):
        k0 = base + t * TILE
        q_pos = q0 + begin + lax.broadcasted_iota(jnp.int32, (1, end - begin), 1)
        return start_of(q_pos) - k0, q_pos - k0

    def scores(raw, t, rows, limits):
        width = raw.shape[1]
        offset = slope2 * (base + t * TILE - q0 - BLOCK // 2).astype(jnp.float32)
        bias = row_bias[rows] + offset
        if not isinstance(limits, tuple):
            k_pos = lax.broadcasted_iota(jnp.int32, (CHUNK, 128), 0) + rows.start
            bias = jnp.where(k_pos >= start0 - (base + t * TILE), bias, -1e30)
        s = raw[rows] * scale2 + jnp.concatenate([bias] * (width // 128), axis=1)
        if limits is None:
            return s
        if not isinstance(limits, tuple):
            return s + limits
        k_pos = lax.broadcasted_iota(jnp.int32, (CHUNK, width), 0) + rows.start
        allowed = jnp.logical_and(k_pos >= limits[0], k_pos <= limits[1])
        return jnp.where(allowed, s, -1e30)

    def weigh(t, limits, top, begin=0, end=BLOCK):
        cols = slice(begin, end)
        raw = mm(k_tile(k_s, t), qt_s[:, cols], NN)
        dp = mm(k_tile(v_s, t), gt_s[:, cols], NN)
        total, delta = total_s[:, cols], delta_s[:, cols]
        for rows in pieces:
            s = scores(raw, t, rows, limits)
            p = jnp.exp2(s if top is None else s - top)
            s_s[kept(t), rows, cols] = p.astype(jnp.bfloat16)
            p_s[kept(t), rows, cols] = dp[rows]
            total = total + folded(p, jnp.sum)
            delta = delta + folded(p * dp[rows], jnp.sum)
        total_s[:, cols] = total
        delta_s[:, cols] = delta

    def clear():
        total_s[...] = jnp.zeros_like(total_s)
        delta_s[...] = jnp.zeros_like(delta_s)

    def shut(width):
        q_pos = q0 + lax.broadcasted_iota(jnp.int32, (1, width), 1)
        return jnp.where(q_pos < first_end, 0.0, -1e30)

    def weigh_tiles(tiles):
        @pl.when(whole)
        def _():
            for t in tiles:
                weigh(t, None, None)

        @pl.when(jnp.logical_not(jnp.logical_or(whole, narrow)))
        def _():
            for t in tiles:
                weigh(t, shut(BLOCK), None)

        @pl.when(narrow)
        def _():
            for t in tiles:
                weigh(t, shut(BLOCK // 2), None, 0, BLOCK // 2)

    def first_pass(i, c):
        at = DIAG // SUB - 1 - i
        arrived(at)
        weigh_tiles((SUB * at + 1, SUB * at))
        return c

    def store(t, dk, dv):
        at = lax.shift_right_logical(t, 10 - SHIFT) if not isinstance(t, int) else t // SUB
        rows = pl.ds(TILE // 128 * (t % SUB), TILE // 128)
        out_s[at, rows, 0] = dk.reshape(TILE // 128, 128, 128)
        out_s[at, rows, 1] = dv.reshape(TILE // 128, 128, 128)

    clear()
    dq_s[...] = jnp.zeros_like(dq_s)
    out_s[5] = jnp.zeros((8, 2, 128, 128), jnp.bfloat16)
    leave(jnp.int32(5))

    def nothing(t, c):
        zero = jnp.zeros((TILE, 128), jnp.bfloat16)
        store(t, zero, zero)
        return c

    lax.fori_loop(0, lo, nothing, 0)

    def leave_block(at, c):
        leave(at)
        return c

    lax.fori_loop(0, lax.shift_right_logical(lo, 10 - SHIFT), leave_block, 0)
    q_copy.wait()
    g_copy.wait()
    qt_s[...] = q_s[...].reshape(BLOCK, 128).T
    gt_s[...] = g_s[...].reshape(BLOCK, 128).T
    arrived(4)
    for i in range(SUB):
        weigh(DIAG + i, masks(DIAG + i, i * TILE), None, i * TILE)
    whole_blocks = lax.shift_right_logical(DIAG - lo, 10 - SHIFT)
    lax.fori_loop(0, whole_blocks, first_pass, 0)

    @pl.when(lo % SUB == 1)
    def _():
        arrived(lax.shift_right_logical(lo, 10 - SHIFT))
        weigh_tiles((lo,))


    total = jnp.sum(total_s[...], axis=0, keepdims=True)
    safe = jnp.logical_and(jnp.max(total) <= 1e30, jnp.min(total) >= 1e-30)

    @pl.when(jnp.logical_not(safe))
    def _():
        m_s[...] = jnp.full_like(m_s, -1e30)

        def highest(t, c):
            raw = mm(k_tile(k_s, t), qt_s[...], NN)
            top = m_s[...]
            for rows in pieces:
                top = jnp.maximum(top, folded(scores(raw, t, rows, masks(t)), jnp.max))
            m_s[...] = top
            return c

        lax.fori_loop(lo, TILES, highest, 0)
        top = jnp.max(m_s[...], axis=0, keepdims=True)
        clear()

        def again(t, c):
            @pl.when(narrow)
            def _():
                half = BLOCK // 2
                weigh(t, masks(t, 0, half), top[:, :half], 0, half)

            @pl.when(jnp.logical_not(narrow))
            def _():
                weigh(t, masks(t), top)

            return c

        lax.fori_loop(lo, DIAG, again, 0)
        for i in range(SUB):
            begin = i * TILE
            weigh(DIAG + i, masks(DIAG + i, begin), top[:, begin:], begin)

    inv = 1.0 / jnp.sum(total_s[...], axis=0, keepdims=True)
    row_delta = jnp.sum(delta_s[...], axis=0, keepdims=True) * inv

    def grads(t, begin=0, end=BLOCK):
        cols = slice(begin, end)
        ws, dss = [], []
        for rows in pieces:
            w = s_s[kept(t), rows, cols].astype(jnp.float32) * inv[:, cols]
            dss.append((w * (p_s[kept(t), rows, cols] - row_delta[:, cols])).astype(jnp.bfloat16))
            ws.append(w.astype(jnp.bfloat16))
        w, ds = jnp.concatenate(ws, axis=0), jnp.concatenate(dss, axis=0)
        g_t = g_s[begin // 128 : end // 128].reshape(end - begin, 128)
        q_t = q_s[begin // 128 : end // 128].reshape(end - begin, 128)
        dv = mm(w, g_t, NN).astype(jnp.bfloat16)
        dk = (mm(ds, q_t, NN) * inv_scale).astype(jnp.bfloat16)
        dq_s[:, cols] += mm(k_tile(k_s, t).T, ds, NN)
        store(t, dk, dv)

    def grads_tiles(tiles, at):
        @pl.when(narrow)
        def _():
            for t in tiles:
                grads(t, 0, BLOCK // 2)

        @pl.when(jnp.logical_not(narrow))
        def _():
            for t in tiles:
                grads(t)

        leave(at)

    def second_pass(i, c):
        at = DIAG // SUB - 1 - i
        grads_tiles((SUB * at, SUB * at + 1), at)
        return c

    for i in range(SUB):
        grads(DIAG + i, i * TILE)
    leave(jnp.int32(4))
    lax.fori_loop(0, whole_blocks, second_pass, 0)

    @pl.when(lo % SUB == 1)
    def _():
        grads_tiles((lo,), lax.shift_right_logical(lo, 10 - SHIFT))

    dq_ref[...] = (dq_s[...] * inv_scale).T.astype(jnp.bfloat16).reshape(8, 128, 128)
    for at in range(6):
        pltpu.make_async_copy(out_s.at[at], mine_refs[0], sems.at[12 + at]).wait()


def attention(doc_lengths, slopes, qg, kvs):
    one = jax.ShapeDtypeStruct((8, 2, 128, 128), jnp.bfloat16)
    late = pltpu.HBM((8, 2, 128, 128), jnp.bfloat16)
    smem = pl.BlockSpec(memory_space=pltpu.SMEM)
    anywhere = pl.BlockSpec(memory_space=pl.ANY)
    vmem = pl.BlockSpec(memory_space=pltpu.VMEM)
    return pl.pallas_call(
        attention_kernel,
        out_shape=(jax.ShapeDtypeStruct((8, 128, 128), jnp.bfloat16),) + (late, late, one) * 2,
        in_specs=[smem, smem] + [anywhere] * 9,
        out_specs=(vmem,) + (anywhere,) * 6,
        scratch_shapes=[
            pltpu.VMEM((8, 128, 128), jnp.bfloat16),
            pltpu.VMEM((8, 128, 128), jnp.bfloat16),
            pltpu.VMEM((40, 128, 128), jnp.bfloat16),
            pltpu.VMEM((40, 128, 128), jnp.bfloat16),
            pltpu.VMEM((128, BLOCK), jnp.bfloat16),
            pltpu.VMEM((128, BLOCK), jnp.bfloat16),
            pltpu.VMEM((TILES - 1, TILE, BLOCK), jnp.bfloat16),
            pltpu.VMEM((TILES - 1, TILE, BLOCK), jnp.float32),
            pltpu.VMEM((8, BLOCK), jnp.float32),
            pltpu.VMEM((8, BLOCK), jnp.float32),
            pltpu.VMEM((8, BLOCK), jnp.float32),
            pltpu.VMEM((128, BLOCK), jnp.float32),
            pltpu.VMEM((6, 8, 2, 128, 128), jnp.bfloat16),
            pltpu.SemaphoreType.DMA((18,)),
        ],
        compiler_params=pltpu.CompilerParams(vmem_limit_bytes=45 * 1024 * 1024),
    )(doc_lengths, slopes, qg, *kvs)


def shifted(x, distance):
    n = lax.axis_size("ctx")
    return lax.ppermute(x, "ctx", [(i, (i + distance) % n) for i in range(n)])


def swapped(x):
    n = lax.axis_size("ctx")
    return lax.ppermute(x, "ctx", [(i, i ^ 1) for i in range(n)])


def routed(x, target):
    n = lax.axis_size("ctx")
    return lax.ppermute(x, "ctx", [(i, target(i)) for i in range(n)])


def up_the_row(i):
    x, y, core = i // 8, i // 2 % 4, i % 2
    return (x * 4 + (y + 1) % 4) * 2 + core


def up_to_two_before(i):
    x, y, core = i // 8, i // 2 % 4, i % 2
    x = (x - 1) % 4 if y in (1, 2) else x
    return (x * 4 + (y + 1) % 4) * 2 + core


def padded(x, before, after):
    return lax.pad(x, jnp.zeros((), x.dtype), ((before, after, 0),) + ((0, 0, 0),) * 3)


def down_the_row(i):
    x, y, core = i // 8, i // 2 % 4, i % 2
    return (x * 4 + (y - 1) % 4) * 2 + core


def down_to_two_after(i):
    x, y, core = i // 8, i // 2 % 4, i % 2
    x = (x + 1) % 4 if y in (1, 2) else x
    return (x * 4 + (y - 1) % 4) * 2 + core


def summed(*parts):
    total = parts[0].astype(jnp.float32)
    for part in parts[1:]:
        total = total + part.astype(jnp.float32)
    return total.astype(jnp.bfloat16)


def to_heads(a, b):
    both = jnp.stack([a.transpose(1, 0, 2), b.transpose(1, 0, 2)], axis=1)
    return lax.all_to_all(both, "head", 0, 0, tiled=True)


def body(queries, keys_in, values, grad_out, slopes, doc_lengths):
    kv = to_heads(keys_in, values)
    qg = to_heads(queries, grad_out)
    one = shifted(kv, 2)
    two_up = shifted(one[:4], 2)
    two_down = routed(routed(kv[4:], down_the_row), down_to_two_after)
    dq, mine, mine_one, mine_two, send, send_one, send_two = attention(
        doc_lengths,
        slopes,
        qg,
        (kv, one, two_up, two_down)
        + (swapped(kv), swapped(one), swapped(two_up), swapped(two_down)),
    )
    other_two = swapped(send_two)
    send_one, send, other_two = lax.optimization_barrier((send_one, send, other_two))
    other_one = swapped(send_one)
    other = swapped(send)
    upper, lower = slice(0, 4), slice(4, 8)
    near = shifted(summed(mine_two[upper], other_two[upper]), -2)
    far = routed(summed(mine_two[lower], other_two[lower]), up_the_row)
    back = shifted(summed(mine_one, other_one, padded(near, 0, 4)), -2)
    far = routed(far, up_to_two_before)
    dkv = summed(mine, other, padded(far, 4, 0))
    dkv, back = lax.optimization_barrier((dkv, back))
    dkv = summed(dkv, back)
    dq = lax.all_to_all(dq, "head", 0, 0, tiled=True)
    dkv = lax.all_to_all(dkv, "head", 0, 0, tiled=True)
    return (
        dq.transpose(1, 0, 2),
        dkv[:, 0].transpose(1, 0, 2),
        dkv[:, 1].transpose(1, 0, 2),
    )


def solution(mesh):
    placed = P(("ctx", "head"), None, None)
    return jax.shard_map(
        body,
        mesh=mesh,
        in_specs=(placed,) * 4 + (P(), P()),
        out_specs=(placed,) * 3,
        check_vma=False,
    )
```
